256 devices in a mesh: outer: 8 (over y, z_lo), inner: 32 (over z_hi, x, core).
Axes of the slice: x: 4, y: 4, z: 8 (z_hi: 4, z_lo: 2; z = z_hi * 2 + z_lo), core: 2. Of those that a mesh axis runs over, the one named last changes fastest.
Arguments:
- queries: bfloat16 [32768, 384], P(('outer', 'inner')), may hold values from -6 to 6
- key_rows: bfloat16 [32768, 128], P(('outer', 'inner')), may hold values from -6 to 6
- value_rows: bfloat16 [32768, 128], P(('outer', 'inner')), may hold values from -6 to 6
- grad_output: bfloat16 [32768, 384], P(('outer', 'inner')), may hold values from -6 to 6
- segments: int32 [32768], replicated, may hold values from 0 to 31, never falling along the last dimension, each value on 1 to 2048 neighbouring positions
Outputs:
- grad_queries: bfloat16 [32768, 384], P(('outer', 'inner'))
- grad_keys: bfloat16 [32768, 128], P(('outer', 'inner'))
- grad_values: bfloat16 [32768, 128], P(('outer', 'inner'))
The draws below stay inside these ranges and needn't reach their ends.
Inputs may be any that keep to these rules, and one draw needn't show every extreme that they name: `segments`: ids never fall; each document has 1 to 2048 tokens and one has exactly 2048.
All inputs are finite; a program needn't handle non-finite values.
Results may differ from the reference program's by a relative error of at most 0.009.
Values may be sent and summed in bfloat16 or wider, within the bound.
A program may use at most 64 MiB of HBM per device.

```python
import math
import jax
import jax.numpy as jnp
import numpy as np
from jax import lax

HD = 128
HEADS = 3
SPAN = 64
DOC_MOST = 2048
TOKENS = 32768
DOCS = 32


def mirrored(natural):
    devices = TOKENS // (2 * SPAN)
    stored = jnp.arange(TOKENS, dtype=jnp.int32)
    device = stored // (2 * SPAN)
    within = stored % (2 * SPAN)
    block_id = jnp.where(within < SPAN, device, 2 * devices - 1 - device)
    return natural[block_id * SPAN + within % SPAN]


def draw_queries(key, part):
    key = jax.random.fold_in(key, 3)
    sample_rows = jnp.clip(jax.random.normal(key, (TOKENS, HEADS * HD)), -6.0, 6.0)
    return mirrored(sample_rows).astype(jnp.bfloat16)


def draw_key_rows(key, part):
    key = jax.random.fold_in(key, 5)
    sample_rows = jnp.clip(jax.random.normal(key, (TOKENS, HD)), -6.0, 6.0)
    return mirrored(sample_rows).astype(jnp.bfloat16)


def block_levels(stream_key, shape, shards, smallest, top_value):
    factor_of, own = 1.0, jax.random.fold_in(stream_key, 6)
    for dim, blocks in shards:
        heights = jnp.exp(jax.random.uniform(jax.random.fold_in(own, dim), (blocks,), jnp.float32, smallest / len(shards), top_value / len(shards)))
        factor_of = factor_of * jnp.repeat(heights, shape[dim] // blocks).reshape([-1 if axis == dim else 1 for axis in range(len(shape))])
    return factor_of


def profile(count, total, bound, lean):
    loads = [(1 << 20) // math.isqrt(rank ** lean) + 1 for rank in range(2, count + 1)]
    spare, counts = total - bound - (count - 1), [1] * (count - 1)
    while spare > 0:
        movable = [i for i in range(count - 1) if counts[i] < bound]
        mass, remaining = sum([loads[i] for i in movable]), spare
        for i in movable:
            addition = min(bound - counts[i], max(1, remaining * loads[i] // mass), spare)
            counts[i] = counts[i] + addition
            spare = spare - addition
    return np.array([bound] + counts)


def uneven(stream_key, number_of, total, limit, skew):
    if number_of == 2:
        one = jax.random.randint(stream_key, (), max(1, total - limit), min(limit, total - 1) + 1)
        return jnp.stack([one, total - one])
    tallies = jnp.asarray(profile(number_of, total, limit, skew), jnp.int32)
    twos = (number_of - 1) // 2
    donor, receiver = tallies[1:1 + 2 * twos:2], tallies[2:2 + 2 * twos:2]
    room = jnp.minimum(donor - 1, limit - receiver)
    moved = jax.random.randint(jax.random.fold_in(stream_key, 1), (twos,), 0, 1 << 20) % (room + 1)
    tallies = tallies.at[1:1 + 2 * twos:2].set(donor - moved).at[2:2 + 2 * twos:2].set(receiver + moved)
    return tallies[jax.random.permutation(jax.random.fold_in(stream_key, 2), number_of)]


def gaussian(key, extent, width, bound, pieces=(), held_as=jnp.bfloat16):
    level = block_levels(key, extent, pieces, -0.22, 0.18) if pieces else 1.0
    values = jax.random.normal(key, extent, jnp.float32) * width * level
    return jnp.minimum(jnp.maximum(values, -bound), bound).astype(held_as)


def setup_inputs(seed: int = 0) -> dict:
    splits = jax.random.split(jax.random.key(seed), 6)
    return {
        "queries": draw_queries(jax.random.fold_in(splits[5], 71), 0),
        "key_rows": draw_key_rows(jax.random.fold_in(splits[5], 71), 0),
        "value_rows": gaussian(splits[2], (TOKENS, HD), 1.0, 6.0, ((0, 256),)),
        "grad_output": gaussian(splits[3], (TOKENS, HEADS * HD), 1.0, 6.0, ((0, 256),)),
        "segments": jnp.searchsorted(jnp.cumsum(uneven(splits[4], DOCS, TOKENS, DOC_MOST, 2)), jnp.arange(TOKENS), side="right").astype(jnp.int32),
    }


def unfold(stored, devices, span_rows):
    shaped = stored.reshape((devices, 2, span_rows) + stored.shape[1:])
    return jnp.concatenate([shaped[:, 0], shaped[::-1, 1]], axis=0).reshape(stored.shape)


def refold(natural, devices, span_rows):
    shaped = natural.reshape((2 * devices, span_rows) + natural.shape[1:])
    stacked = jnp.stack([shaped[:devices], shaped[devices:][::-1]], axis=1)
    return stacked.reshape(natural.shape)


def reference(queries, key_rows, value_rows, grad_output, segments):
    span_rows = SPAN
    devices = TOKENS // (2 * span_rows)
    head_width = HD
    head_count = HEADS
    score_scale = head_width ** -0.5
    window = DOC_MOST + span_rows
    query_nat = unfold(queries, devices, span_rows).reshape(TOKENS, head_count, head_width)
    grad_nat = unfold(grad_output, devices, span_rows).reshape(TOKENS, head_count, head_width)
    key_nat = unfold(key_rows, devices, span_rows)
    value_nat = unfold(value_rows, devices, span_rows)
    pad_keys = jnp.concatenate([jnp.zeros((DOC_MOST, head_width), key_rows.dtype), key_nat])
    pad_values = jnp.concatenate([jnp.zeros((DOC_MOST, head_width), value_rows.dtype), value_nat])
    seg_nat = segments.astype(jnp.int32)
    pad_seg = jnp.concatenate([jnp.full((DOC_MOST,), -1, jnp.int32), seg_nat])
    pad_pos = jnp.arange(TOKENS + DOC_MOST, dtype=jnp.int32) - DOC_MOST

    def block_step(carry, block):
        grad_keys_pad, grad_values_pad = carry
        start = (block * span_rows).astype(jnp.int32)
        query_block = lax.dynamic_slice_in_dim(query_nat, start, span_rows, 0).astype(jnp.float32)
        grad_block = lax.dynamic_slice_in_dim(grad_nat, start, span_rows, 0).astype(jnp.float32)
        query_seg = lax.dynamic_slice_in_dim(seg_nat, start, span_rows, 0)
        query_pos = start + jnp.arange(span_rows, dtype=jnp.int32)
        key_win = lax.dynamic_slice_in_dim(pad_keys, start, window, 0).astype(jnp.float32)
        value_win = lax.dynamic_slice_in_dim(pad_values, start, window, 0).astype(jnp.float32)
        seg_win = lax.dynamic_slice_in_dim(pad_seg, start, window, 0)
        pos_win = lax.dynamic_slice_in_dim(pad_pos, start, window, 0)
        allowed = (seg_win[None, :] == query_seg[:, None]) & (pos_win[None, :] <= query_pos[:, None])
        scores = jnp.einsum("qhd,kd->hqk", query_block, key_win) * score_scale
        masked = jnp.where(allowed[None], scores, -jnp.inf)
        top_score = jnp.max(masked, axis=2, keepdims=True)
        total = jnp.sum(jnp.where(allowed[None], jnp.exp(scores - top_score), 0.0), axis=2, keepdims=True)
        log_total = top_score + jnp.log(total)
        attn_probs = jnp.where(allowed[None], jnp.exp(scores - log_total), 0.0)
        slopes = jnp.einsum("qhd,kd->hqk", grad_block, value_win)
        delta_rows = jnp.sum(attn_probs * slopes, axis=2, keepdims=True)
        grad_scores = attn_probs * (slopes - delta_rows)
        probs_low = lax.optimization_barrier(attn_probs.astype(jnp.bfloat16)).astype(jnp.float32)
        grad_low = lax.optimization_barrier(grad_scores.astype(jnp.bfloat16)).astype(jnp.float32)
        grad_query = (jnp.einsum("hqk,kd->qhd", grad_low, key_win) * score_scale).astype(jnp.bfloat16)
        key_add = jnp.einsum("hqk,qhd->kd", grad_low, query_block) * score_scale
        value_add = jnp.einsum("hqk,qhd->kd", probs_low, grad_block)
        old_keys = lax.dynamic_slice_in_dim(grad_keys_pad, start, window, 0)
        old_values = lax.dynamic_slice_in_dim(grad_values_pad, start, window, 0)
        grad_keys_pad = lax.dynamic_update_slice_in_dim(grad_keys_pad, old_keys + key_add, start, 0)
        grad_values_pad = lax.dynamic_update_slice_in_dim(grad_values_pad, old_values + value_add, start, 0)
        return (grad_keys_pad, grad_values_pad), grad_query

    start_carry = (jnp.zeros((TOKENS + DOC_MOST, head_width), jnp.float32), jnp.zeros((TOKENS + DOC_MOST, head_width), jnp.float32))
    blocks = jnp.arange(TOKENS // span_rows, dtype=jnp.int32)
    (grad_keys_pad, grad_values_pad), grad_query_blocks = lax.scan(block_step, start_carry, blocks)
    grad_query_nat = grad_query_blocks.reshape(TOKENS, head_count * head_width)
    grad_keys_nat = grad_keys_pad[DOC_MOST:].astype(jnp.bfloat16)
    grad_values_nat = grad_values_pad[DOC_MOST:].astype(jnp.bfloat16)
    return (refold(grad_query_nat, devices, span_rows), refold(grad_keys_nat, devices, span_rows), refold(grad_values_nat, devices, span_rows))
```

```python
import functools
import math

import jax
import jax.numpy as jnp
from jax import lax
from jax.experimental import pallas as pl
from jax.experimental.pallas import tpu as pltpu
from jax.sharding import PartitionSpec as P

MESH = pl.DeviceIdType.MESH
NEGATIVE = -1e30
HD = 128
HEADS = 3
SPAN = 64
CHUNK = 512
WINDOW = 5
QTILE = 256
QSTEPS = HEADS * (CHUNK // QTILE)
SCALE = HD**-0.5
KAPPA = SCALE * math.log2(math.e)
f32 = jnp.float32
bf16 = jnp.bfloat16


def dot(a, b, dims):
    return lax.dot_general(a, b, ((dims[0], dims[1]), ((), ())), preferred_element_type=f32)


def kernel(
    slabs_per_group,
    slabs,
    docs,
    q_hbm,
    k_hbm,
    v_hbm,
    g_hbm,
    seg_hbm,
    dq_out,
    dk_out,
    dv_out,
    qd,
    qd_other,
    kv,
    kv_other,
    seg,
    bias,
    e_buf,
    dp_buf,
    ds_buf,
    stat,
    dq_send,
    dq_recv,
    dkv_own,
    dkv_send,
    dkv_recv,
    fin_send,
    fin_recv,
    local_sem,
    seg_sem,
    qd_send_sem,
    qd_recv_sem,
    swap_send_sem,
    swap_recv_sem,
    kv_send_sem,
    kv_recv_sem,
    stat_send_sem,
    stat_recv_sem,
    dq_send_sem,
    dq_recv_sem,
    dkv_send_sem,
    dkv_recv_sem,
    fin_send_sem,
    fin_recv_sem,
):
    chunks = 2 * slabs
    group = lax.axis_index("outer")
    inner = lax.axis_index("inner")
    place = inner % 8
    base = inner - place
    slab = group * slabs_per_group + inner // 8
    x = place // 2
    core = place % 2
    is_back = x // 2
    unit = jnp.where(is_back == 1, 3 - x, x)
    chunk = jnp.where(is_back == 1, chunks - 1 - slab, slab)

    def in_slab(place_to):
        return (group, base + place_to)

    def holder(chunk_to):
        back = chunk_to // slabs
        slab_to = jnp.where(back == 1, chunks - 1 - chunk_to, chunk_to)
        x_to = jnp.where(back == 1, 3 - unit, unit)
        return (
            slab_to // slabs_per_group,
            (slab_to % slabs_per_group) * 8 + x_to * 2 + core,
        )

    def block_of(place_of, back):
        return jnp.where(back == 1, 7 - place_of, place_of)

    def rows_of(block):
        return pl.ds(pl.multiple_of(block * SPAN, SPAN), SPAN)

    sibling = place + 1 - 2 * core
    partner = (3 - x) * 2 + core
    mate = (x + 1 - 2 * (x % 2)) * 2 + core
    far = (3 - (x + 1 - 2 * (x % 2))) * 2 + core
    own_block = block_of(place, is_back)
    own_rows = pl.ds(pl.multiple_of(is_back * SPAN, SPAN), SPAN)
    other_rows = pl.ds(pl.multiple_of((1 - is_back) * SPAN, SPAN), SPAN)

    locals_ = [
        pltpu.make_async_copy(k_hbm.at[own_rows], kv.at[0, 0, 0], local_sem.at[0]),
        pltpu.make_async_copy(v_hbm.at[own_rows], kv.at[0, 0, 1], local_sem.at[1]),
        pltpu.make_async_copy(k_hbm.at[other_rows], kv_other.at[0], local_sem.at[2]),
        pltpu.make_async_copy(v_hbm.at[other_rows], kv_other.at[1], local_sem.at[3]),
        pltpu.make_async_copy(q_hbm.at[other_rows], qd_other.at[0], local_sem.at[4]),
        pltpu.make_async_copy(g_hbm.at[other_rows], qd_other.at[1], local_sem.at[5]),
        pltpu.make_async_copy(q_hbm.at[own_rows], qd.at[0, rows_of(own_block)], local_sem.at[6]),
        pltpu.make_async_copy(g_hbm.at[own_rows], qd.at[1, rows_of(own_block)], local_sem.at[7]),
    ]
    for copy in locals_:
        copy.start()
    seg_copy = pltpu.make_async_copy(seg_hbm, seg, seg_sem)
    seg_copy.start()

    barrier = pltpu.get_barrier_semaphore()
    for step in range(1, 8):
        pl.semaphore_signal(
            barrier, inc=1, device_id=in_slab((place + step) % 8), device_id_type=MESH
        )
    for k in range(1, WINDOW):
        for to, there in ((chunk + k, chunk + k < chunks), (chunk - k, chunk - k >= 0)):

            @pl.when(there)
            def _():
                pl.semaphore_signal(barrier, inc=1, device_id=holder(to), device_id_type=MESH)

    later = jnp.minimum(chunks - 1 - chunk, WINDOW - 1)
    earlier = jnp.minimum(chunk, WINDOW - 1)
    for copy in locals_:
        copy.wait()
    pl.semaphore_wait(barrier, 7 + later + earlier)

    def send(src, dst, send_sem, recv_sem, to):
        copy = pltpu.make_async_remote_copy(
            src_ref=src,
            dst_ref=dst,
            send_sem=send_sem,
            recv_sem=recv_sem,
            device_id=to,
            device_id_type=MESH,
        )
        copy.start()
        return copy

    def arrived(dst, recv_sem):
        pltpu.make_async_copy(dst, dst, recv_sem).wait()

    def qd_block(block):
        return qd.at[:, rows_of(block)]

    def send_block(src, block, sem, to):
        return send(src, qd_block(block), qd_send_sem.at[sem], qd_recv_sem.at[block], in_slab(to))

    sent = []
    sent.append(send(kv_other, kv.at[0, 1], swap_send_sem, swap_recv_sem, in_slab(partner)))

    def kv_copy(k, half):
        return pltpu.make_async_remote_copy(
            src_ref=kv.at[0, half],
            dst_ref=kv.at[k, half],
            send_sem=kv_send_sem.at[k, half],
            recv_sem=kv_recv_sem.at[k, half],
            device_id=holder(chunk + k),
            device_id_type=MESH,
        )

    def kv_start(half):
        for k in range(1, WINDOW):

            @pl.when(chunk + k < chunks)
            def _():
                kv_copy(k, half).start()

    other_block = block_of(place, 1 - is_back)
    sent.append(send_block(qd_other, other_block, 0, far))
    sent.append(send_block(qd_block(own_block), own_block, 1, mate))
    sent.append(send_block(qd_other, other_block, 2, partner))
    kv_start(0)
    sent.append(send_block(qd_block(own_block), own_block, 3, sibling))

    for k in range(1, WINDOW):

        @pl.when(chunk - k < 0)
        def _():
            kv[k] = jnp.zeros(kv.shape[1:], bf16)

    seg_copy.wait()
    doc_ids = lax.broadcasted_iota(jnp.int32, (docs, 128), 0)

    def count(i, acc):
        rows = seg[pl.ds(pl.multiple_of(i * 8, 8), 8), :]
        for r in range(8):
            acc = acc + jnp.where(rows[r : r + 1, :] < doc_ids, 1.0, 0.0)
        return acc

    tally = lax.fori_loop(0, seg.shape[0] // 8, count, jnp.zeros((docs, 128), f32))
    firsts = jnp.sum(tally, axis=1, keepdims=True)
    query_pos = (lax.broadcasted_iota(jnp.int32, (1, CHUNK), 1) + chunk * CHUNK).astype(f32)
    starts = jnp.max(jnp.where(firsts <= query_pos, firsts, 0.0), axis=0, keepdims=True)
    row_ids = lax.broadcasted_iota(jnp.int32, (SPAN, QTILE), 0)
    for k in range(WINDOW):
        key_chunk = chunk - k
        back = (key_chunk + slabs) // slabs - 1
        for half in range(2):
            front_place = jnp.where(half == 0, unit, 3 - unit) * 2 + core
            back_place = jnp.where(half == 0, 3 - unit, unit) * 2 + core
            block = jnp.where(back == 1, 7 - back_place, front_place)
            key_pos = (row_ids + (key_chunk * CHUNK + block * SPAN)).astype(f32)
            for part in range(CHUNK // QTILE):
                lanes = slice(part * QTILE, (part + 1) * QTILE)
                allowed = (key_pos >= starts[:, lanes]) & (key_pos <= query_pos[:, lanes])
                at = (2 * k + half) * SPAN
                bias[part, at : at + SPAN, :] = jnp.where(allowed, 0.0, NEGATIVE)

    arrived(kv.at[0, 1], swap_recv_sem)
    kv_start(1)
    for sem, source in ((4, mate), (5, partner), (6, far)):
        block = block_of(source, is_back)
        arrived(qd_block(block), qd_recv_sem.at[block])
        sent.append(send_block(qd_block(block), block, sem, sibling))
    for step in range(4):
        block = block_of((sibling + 2 * step) % 8, is_back)
        arrived(qd_block(block), qd_recv_sem.at[block])
    for k in range(1, WINDOW):

        @pl.when(chunk - k >= 0)
        def _():
            for half in range(2):
                arrived(kv.at[k, half], kv_recv_sem.at[k, half])

    def tile(n):
        head = n // 2
        part = n % 2
        return (
            part,
            pl.ds(pl.multiple_of(part * QTILE, QTILE), QTILE),
            pl.ds(pl.multiple_of(head * HD, HD), HD),
        )

    def keys_of(k):
        return kv[k, :, 0].reshape(2 * SPAN, HD)

    def values_of(k):
        return kv[k, :, 1].reshape(2 * SPAN, HD)

    shard = 2 * unit + core

    def forward(n, carry):
        part, rows, lanes = tile(n)
        q = qd[0, rows, lanes]
        g = qd[1, rows, lanes]
        top = jnp.full((1, QTILE), NEGATIVE, f32)
        for k in range(WINDOW):
            at = slice(2 * SPAN * k, 2 * SPAN * (k + 1))
            s = dot(keys_of(k), q, ((1,), (1,))) + bias[part, at, :]
            e_buf[n, at, :] = s
            top = jnp.maximum(top, jnp.max(s, axis=0, keepdims=True))
        total = jnp.zeros((1, QTILE), f32)
        slope = jnp.zeros((1, QTILE), f32)
        for k in range(WINDOW):
            at = slice(2 * SPAN * k, 2 * SPAN * (k + 1))
            dp = dot(values_of(k), g, ((1,), (1,)))
            e = jnp.exp2((e_buf[n, at, :] - top) * KAPPA)
            e_buf[n, at, :] = e
            dp_buf[n, at, :] = dp
            total = total + jnp.sum(e, axis=0, keepdims=True)
            slope = slope + jnp.sum(e * dp, axis=0, keepdims=True)
        stat[shard, n, 0:1, :] = top
        stat[shard, n, 1:2, :] = total
        stat[shard, n, 2:3, :] = slope
        return carry

    stat[shard] = jnp.zeros(stat.shape[1:], f32)
    lax.fori_loop(0, QSTEPS, forward, 0)

    for sem, to in ((0, mate), (1, sibling), (2, mate + 1 - 2 * core)):
        sent.append(
            send(
                stat.at[shard],
                stat.at[shard],
                stat_send_sem.at[sem],
                stat_recv_sem.at[shard],
                in_slab(to),
            )
        )
    for step in range(1, 4):
        peer = (shard + step) % 4
        arrived(stat.at[peer], stat_recv_sem.at[peer])

    tops = stat[:, :, 0:1, :]
    top = jnp.max(tops, axis=0)
    factors = jnp.exp2((tops - top[None]) * KAPPA)
    total = jnp.sum(stat[:, :, 1:2, :] * factors, axis=0)
    delta = jnp.sum(stat[:, :, 2:3, :] * factors, axis=0) / total
    ratio = jnp.exp2((stat[shard, :, 0:1, :] - top) * KAPPA) / total

    def dkv_copy(k):
        return pltpu.make_async_remote_copy(
            src_ref=dkv_send.at[k],
            dst_ref=dkv_recv.at[k],
            send_sem=dkv_send_sem.at[k],
            recv_sem=dkv_recv_sem.at[k],
            device_id=holder(chunk - k),
            device_id_type=MESH,
        )

    for k in (4, 3, 2, 1, 0):
        at = slice(2 * SPAN * k, 2 * SPAN * (k + 1))
        dk = jnp.zeros((2 * SPAN, HD), f32)
        dv = jnp.zeros((2 * SPAN, HD), f32)
        for n in range(QSTEPS):
            head, part = n // 2, n % 2
            rows = slice(part * QTILE, (part + 1) * QTILE)
            lanes = slice(head * HD, (head + 1) * HD)
            p = e_buf[n, at, :] * ratio[n]
            ds = (p * (dp_buf[n, at, :] - delta[n])).astype(bf16)
            ds_buf[n, at, :] = ds
            dv = dv + dot(p.astype(bf16), qd[1, rows, lanes], ((1,), (0,)))
            dk = dk + dot(ds, qd[0, rows, lanes], ((1,), (0,)))
        dk = dk * SCALE
        if k == 0:
            dkv_own[:, 0] = dk.reshape(2, SPAN, HD)
            dkv_own[:, 1] = dv.reshape(2, SPAN, HD)
        else:
            dkv_send[k, :, 0] = dk.astype(bf16).reshape(2, SPAN, HD)
            dkv_send[k, :, 1] = dv.astype(bf16).reshape(2, SPAN, HD)

            @pl.when(chunk - k >= 0)
            def _():
                dkv_copy(k).start()

    keys = kv[:, :, 0].reshape(2 * SPAN * WINDOW, HD)
    for n in range(QSTEPS):
        head, part = n // 2, n % 2
        dqt = dot(keys, ds_buf[n], ((0,), (0,)))
        dq_send[part * QTILE : (part + 1) * QTILE, head * HD : (head + 1) * HD] = (
            dqt.T * SCALE
        ).astype(bf16)
    for step in (4, 2, 6, 3, 5, 7, 1):
        to = (place + step) % 8
        sent.append(
            send(
                dq_send.at[rows_of(block_of(to, is_back))],
                dq_recv.at[is_back, shard],
                dq_send_sem.at[step],
                dq_recv_sem.at[is_back, shard],
                in_slab(to),
            )
        )
    dq_recv[is_back, shard] = dq_send[rows_of(own_block), :]

    for k in range(1, WINDOW):

        @pl.when(chunk + k < chunks)
        def _():
            arrived(dkv_recv.at[k], dkv_recv_sem.at[k])
            dkv_own[...] = dkv_own[...] + dkv_recv[k].astype(f32)

    fin_send[...] = dkv_own[1].astype(bf16)
    sent.append(send(fin_send, fin_recv, fin_send_sem, fin_recv_sem, in_slab(partner)))
    dk_out[own_rows, :] = dkv_own[0, 0].astype(bf16)
    dv_out[own_rows, :] = dkv_own[0, 1].astype(bf16)

    for step in range(1, 8):
        source = (place + step) % 8
        source_x = source // 2
        source_back = source_x // 2
        source_unit = jnp.where(source_back == 1, 3 - source_x, source_x)
        source_shard = 2 * source_unit + source % 2
        arrived(
            dq_recv.at[source_back, source_shard], dq_recv_sem.at[source_back, source_shard]
        )
    for back in range(2):
        total_dq = dq_recv[back, 0].astype(f32)
        for j in range(1, 4):
            total_dq = total_dq + dq_recv[back, j].astype(f32)
        dq_out[back * SPAN : (back + 1) * SPAN, :] = total_dq.astype(bf16)
    arrived(fin_recv, fin_recv_sem)
    dk_out[other_rows, :] = fin_recv[0]
    dv_out[other_rows, :] = fin_recv[1]

    for copy in sent:
        copy.wait_send()
    for k in range(1, WINDOW):

        @pl.when(chunk + k < chunks)
        def _():
            for half in range(2):
                kv_copy(k, half).wait_send()

        @pl.when(chunk - k >= 0)
        def _():
            dkv_copy(k).wait_send()


def local(queries, key_rows, value_rows, grad_output, segments):
    groups = lax.axis_size("outer")
    slabs_per_group = lax.axis_size("inner") // 8
    slabs = groups * slabs_per_group
    rows = queries.shape[0]
    positions = segments.shape[0]
    vmem = pltpu.VMEM
    sem = pltpu.SemaphoreType.DMA
    keys = 2 * SPAN * WINDOW
    return pl.pallas_call(
        functools.partial(kernel, slabs_per_group, slabs, 32),
        out_shape=(
            jax.ShapeDtypeStruct((rows, HEADS * HD), bf16),
            jax.ShapeDtypeStruct((rows, HD), bf16),
            jax.ShapeDtypeStruct((rows, HD), bf16),
        ),
        in_specs=[pl.BlockSpec(memory_space=pl.ANY)] * 5,
        out_specs=[pl.BlockSpec(memory_space=pltpu.VMEM)] * 3,
        scratch_shapes=[
            vmem((2, CHUNK, HEADS * HD), bf16),
            vmem((2, SPAN, HEADS * HD), bf16),
            vmem((WINDOW, 2, 2, SPAN, HD), bf16),
            vmem((2, SPAN, HD), bf16),
            vmem((positions // 128, 128), jnp.int32),
            vmem((CHUNK // QTILE, keys, QTILE), f32),
            vmem((QSTEPS, keys, QTILE), f32),
            vmem((QSTEPS, keys, QTILE), f32),
            vmem((QSTEPS, keys, QTILE), bf16),
            vmem((4, QSTEPS, 8, QTILE), f32),
            vmem((CHUNK, HEADS * HD), bf16),
            vmem((2, 4, SPAN, HEADS * HD), bf16),
            vmem((2, 2, SPAN, HD), f32),
            vmem((WINDOW, 2, 2, SPAN, HD), bf16),
            vmem((WINDOW, 2, 2, SPAN, HD), bf16),
            vmem((2, SPAN, HD), bf16),
            vmem((2, SPAN, HD), bf16),
            sem((8,)),
            sem,
            sem((7,)),
            sem((8,)),
            sem,
            sem,
            sem((WINDOW, 2)),
            sem((WINDOW, 2)),
            sem((3,)),
            sem((4,)),
            sem((8,)),
            sem((2, 4)),
            sem((WINDOW,)),
            sem((WINDOW,)),
            sem,
            sem,
        ],
        compiler_params=pltpu.CompilerParams(
            collective_id=0, has_side_effects=True, vmem_limit_bytes=40 * 1024 * 1024
        ),
        name="windowed_backward",
    )(queries, key_rows, value_rows, grad_output, segments.reshape(positions // 128, 128))


def solution(mesh):
    placed = P(("outer", "inner"), None)
    return jax.shard_map(
        local,
        mesh=mesh,
        in_specs=(placed, placed, placed, placed, P()),
        out_specs=(placed, placed, placed),
        check_vma=False,
    )
```

```python
import functools
import math

import jax
import jax.numpy as jnp
from jax import lax
from jax.experimental import pallas as pl
from jax.experimental.pallas import tpu as pltpu
from jax.sharding import PartitionSpec as P

MESH = pl.DeviceIdType.MESH
NEGATIVE = -1e30
TINY = 1e-30
HD = 128
HEADS = 3
SPAN = 64
CHUNK = 512
WINDOW = 5
QTILE = 256
QSTEPS = HEADS * (CHUNK // QTILE)
SCALE = HD**-0.5
KAPPA = SCALE * math.log2(math.e)
f32 = jnp.float32
bf16 = jnp.bfloat16


def dot(a, b, dims):
    return lax.dot_general(a, b, ((dims[0], dims[1]), ((), ())), preferred_element_type=f32)


def kernel(
    slabs_per_group,
    slabs,
    docs,
    q_hbm,
    k_hbm,
    v_hbm,
    g_hbm,
    seg_hbm,
    dq_out,
    dk_out,
    dv_out,
    qd,
    qd_other,
    kv,
    kv_other,
    seg,
    bias,
    e_buf,
    dp_buf,
    ds_buf,
    stat,
    dq_send,
    dq_recv,
    dkv_own,
    dkv_send,
    dkv_recv,
    local_sem,
    seg_sem,
    qd_send_sem,
    qd_recv_sem,
    swap_send_sem,
    swap_recv_sem,
    kv_send_sem,
    kv_recv_sem,
    stat_send_sem,
    stat_recv_sem,
    dq_send_sem,
    dq_recv_sem,
    dkv_send_sem,
    dkv_recv_sem,
):
    chunks = 2 * slabs
    group = lax.axis_index("outer")
    inner = lax.axis_index("inner")
    place = inner % 8
    base = inner - place
    slab = group * slabs_per_group + inner // 8
    x = place // 2
    core = place % 2
    is_back = x // 2
    unit = jnp.where(is_back == 1, 3 - x, x)
    chunk = jnp.where(is_back == 1, chunks - 1 - slab, slab)
    other_chunk = chunks - 1 - chunk

    def in_slab(place_to):
        return (group, base + place_to)

    def holder(chunk_to, half=0):
        back = chunk_to // slabs
        slab_to = jnp.where(back == 1, chunks - 1 - chunk_to, chunk_to)
        x_to = jnp.where((back + half) % 2 == 1, 3 - unit, unit)
        return (
            slab_to // slabs_per_group,
            (slab_to % slabs_per_group) * 8 + x_to * 2 + core,
        )

    def block_of(place_of, back):
        return jnp.where(back == 1, 7 - place_of, place_of)

    def rows_of(block):
        return pl.ds(pl.multiple_of(block * SPAN, SPAN), SPAN)

    sibling = place + 1 - 2 * core
    partner = (3 - x) * 2 + core
    mate = (x + 1 - 2 * (x % 2)) * 2 + core
    far = (3 - (x + 1 - 2 * (x % 2))) * 2 + core
    own_block = block_of(place, is_back)
    own_rows = pl.ds(pl.multiple_of(is_back * SPAN, SPAN), SPAN)
    other_rows = pl.ds(pl.multiple_of((1 - is_back) * SPAN, SPAN), SPAN)

    locals_ = [
        pltpu.make_async_copy(k_hbm.at[own_rows], kv.at[0, 0, 0], local_sem.at[0]),
        pltpu.make_async_copy(v_hbm.at[own_rows], kv.at[0, 0, 1], local_sem.at[1]),
        pltpu.make_async_copy(k_hbm.at[other_rows], kv_other.at[0], local_sem.at[2]),
        pltpu.make_async_copy(v_hbm.at[other_rows], kv_other.at[1], local_sem.at[3]),
        pltpu.make_async_copy(q_hbm.at[other_rows], qd_other.at[0], local_sem.at[4]),
        pltpu.make_async_copy(g_hbm.at[other_rows], qd_other.at[1], local_sem.at[5]),
        pltpu.make_async_copy(q_hbm.at[own_rows], qd.at[0, rows_of(own_block)], local_sem.at[6]),
        pltpu.make_async_copy(g_hbm.at[own_rows], qd.at[1, rows_of(own_block)], local_sem.at[7]),
    ]
    for copy in locals_:
        copy.start()
    seg_copy = pltpu.make_async_copy(seg_hbm, seg, seg_sem)
    seg_copy.start()

    barrier = pltpu.get_barrier_semaphore()
    for step in range(1, 8):
        pl.semaphore_signal(
            barrier, inc=1, device_id=in_slab((place + step) % 8), device_id_type=MESH
        )
    for k in range(1, WINDOW):
        for to, half, there in (
            (chunk + k, 0, chunk + k < chunks),
            (chunk - k, 0, chunk - k >= 0),
            (other_chunk + k, 0, (other_chunk + k < chunks) & (other_chunk + k != chunk)),
            (chunk - k, 1, (chunk - k >= 0) & (chunk - k != other_chunk)),
        ):

            @pl.when(there)
            def _():
                pl.semaphore_signal(
                    barrier, inc=1, device_id=holder(to, half), device_id_type=MESH
                )

    later = jnp.minimum(chunks - 1 - chunk, WINDOW - 1)
    earlier = jnp.minimum(chunk, WINDOW - 1)
    apart = chunk - other_chunk
    own_second = jnp.where((apart > 0) & (apart < WINDOW), 1, 0)
    for copy in locals_:
        copy.wait()
    pl.semaphore_wait(barrier, 7 + later + 3 * earlier - 2 * own_second)

    def send(src, dst, send_sem, recv_sem, to):
        copy = pltpu.make_async_remote_copy(
            src_ref=src,
            dst_ref=dst,
            send_sem=send_sem,
            recv_sem=recv_sem,
            device_id=to,
            device_id_type=MESH,
        )
        copy.start()
        return copy

    def arrived(dst, recv_sem):
        pltpu.make_async_copy(dst, dst, recv_sem).wait()

    def qd_block(block):
        return qd.at[:, rows_of(block)]

    def send_block(src, block, sem, to):
        return send(src, qd_block(block), qd_send_sem.at[sem], qd_recv_sem.at[block], in_slab(to))

    sent = []
    sent.append(send(kv_other, kv.at[0, 1], swap_send_sem, swap_recv_sem, in_slab(partner)))

    def kv_copy(k, half):
        return pltpu.make_async_remote_copy(
            src_ref=kv.at[0, half],
            dst_ref=kv.at[k, half],
            send_sem=kv_send_sem.at[k, half],
            recv_sem=kv_recv_sem.at[k, half],
            device_id=holder(chunk + k),
            device_id_type=MESH,
        )

    def kv_start(half):
        for k in range(1, WINDOW):

            @pl.when(chunk + k < chunks)
            def _():
                kv_copy(k, half).start()

    other_block = block_of(place, 1 - is_back)
    sent.append(send_block(qd_other, other_block, 0, far))
    sent.append(send_block(qd_block(own_block), own_block, 1, mate))
    sent.append(send_block(qd_other, other_block, 2, partner))
    kv_start(0)
    sent.append(send_block(qd_block(own_block), own_block, 3, sibling))

    for k in range(1, WINDOW):

        @pl.when(chunk - k < 0)
        def _():
            kv[k] = jnp.zeros(kv.shape[1:], bf16)

    seg_copy.wait()
    doc_ids = lax.broadcasted_iota(jnp.int32, (docs, 128), 0)

    def count(i, acc):
        rows = seg[pl.ds(pl.multiple_of(i * 8, 8), 8), :]
        for r in range(8):
            acc = acc + jnp.where(rows[r : r + 1, :] < doc_ids, 1.0, 0.0)
        return acc

    tally = lax.fori_loop(0, seg.shape[0] // 8, count, jnp.zeros((docs, 128), f32))
    firsts = jnp.sum(tally, axis=1, keepdims=True)
    query_pos = (lax.broadcasted_iota(jnp.int32, (1, CHUNK), 1) + chunk * CHUNK).astype(f32)
    starts = jnp.max(jnp.where(firsts <= query_pos, firsts, 0.0), axis=0, keepdims=True)
    row_ids = lax.broadcasted_iota(jnp.int32, (SPAN, QTILE), 0)
    for k in range(WINDOW):
        key_chunk = chunk - k
        back = (key_chunk + slabs) // slabs - 1
        for half in range(2):
            front_place = jnp.where(half == 0, unit, 3 - unit) * 2 + core
            back_place = jnp.where(half == 0, 3 - unit, unit) * 2 + core
            block = jnp.where(back == 1, 7 - back_place, front_place)
            key_pos = (row_ids + (key_chunk * CHUNK + block * SPAN)).astype(f32)
            for part in range(CHUNK // QTILE):
                lanes = slice(part * QTILE, (part + 1) * QTILE)
                allowed = (key_pos >= starts[:, lanes]) & (key_pos <= query_pos[:, lanes])
                at = (2 * k + half) * SPAN
                bias[part, at : at + SPAN, :] = jnp.where(allowed, 0.0, NEGATIVE)

    arrived(kv.at[0, 1], swap_recv_sem)
    kv_start(1)
    for sem, source in ((4, mate), (5, partner), (6, far)):
        block = block_of(source, is_back)
        arrived(qd_block(block), qd_recv_sem.at[block])
        sent.append(send_block(qd_block(block), block, sem, sibling))
    for step in range(4):
        block = block_of((sibling + 2 * step) % 8, is_back)
        arrived(qd_block(block), qd_recv_sem.at[block])
    for k in range(1, WINDOW):

        @pl.when(chunk - k >= 0)
        def _():
            for half in range(2):
                arrived(kv.at[k, half], kv_recv_sem.at[k, half])

    def tile(n):
        head = n // 2
        part = n % 2
        return (
            part,
            pl.ds(pl.multiple_of(part * QTILE, QTILE), QTILE),
            pl.ds(pl.multiple_of(head * HD, HD), HD),
        )

    def keys_of(k):
        return kv[k, :, 0].reshape(2 * SPAN, HD)

    def values_of(k):
        return kv[k, :, 1].reshape(2 * SPAN, HD)

    shard = 2 * unit + core

    def forward(n, carry):
        part, rows, lanes = tile(n)
        q = qd[0, rows, lanes]
        g = qd[1, rows, lanes]
        top = jnp.full((1, QTILE), NEGATIVE, f32)
        for k in range(WINDOW):
            at = slice(2 * SPAN * k, 2 * SPAN * (k + 1))
            s = dot(keys_of(k), q, ((1,), (1,))) + bias[part, at, :]
            e_buf[n, at, :] = s
            top = jnp.maximum(top, jnp.max(s, axis=0, keepdims=True))
        total = jnp.zeros((1, QTILE), f32)
        slope = jnp.zeros((1, QTILE), f32)
        for k in range(WINDOW):
            at = slice(2 * SPAN * k, 2 * SPAN * (k + 1))
            dp = dot(values_of(k), g, ((1,), (1,)))
            e = jnp.exp2((e_buf[n, at, :] - top) * KAPPA)
            e_buf[n, at, :] = e
            dp_buf[n, at, :] = dp
            total = total + jnp.sum(e, axis=0, keepdims=True)
            slope = slope + jnp.sum(e * dp, axis=0, keepdims=True)
        stat[shard, 0, pl.ds(n, 1), :] = top
        stat[shard, 1, pl.ds(n, 1), :] = total
        stat[shard, 2, pl.ds(n, 1), :] = slope
        return carry

    stat[shard] = jnp.zeros(stat.shape[1:], f32)
    lax.fori_loop(0, QSTEPS, forward, 0)

    for sem, to in ((0, mate), (1, sibling), (2, mate + 1 - 2 * core)):
        sent.append(
            send(
                stat.at[shard],
                stat.at[shard],
                stat_send_sem.at[sem],
                stat_recv_sem.at[shard],
                in_slab(to),
            )
        )
    for step in range(1, 4):
        peer = (shard + step) % 4
        arrived(stat.at[peer], stat_recv_sem.at[peer])

    tops = stat[:, 0]
    top = jnp.max(tops, axis=0)
    factors = jnp.exp2((tops - top[None]) * KAPPA)
    inverse = 1.0 / jnp.maximum(jnp.sum(stat[:, 1] * factors, axis=0), TINY)
    delta = jnp.sum(stat[:, 2] * factors, axis=0) * inverse
    ratio = jnp.exp2((stat[shard, 0] - top) * KAPPA) * inverse

    def dkv_copy(k, half):
        return pltpu.make_async_remote_copy(
            src_ref=dkv_send.at[k, half],
            dst_ref=dkv_recv.at[half, k],
            send_sem=dkv_send_sem.at[half, k],
            recv_sem=dkv_recv_sem.at[half, k],
            device_id=holder(chunk - k, half),
            device_id_type=MESH,
        )

    for k in (4, 3, 2, 1, 0):
        at = slice(2 * SPAN * k, 2 * SPAN * (k + 1))
        dk = jnp.zeros((2 * SPAN, HD), f32)
        dv = jnp.zeros((2 * SPAN, HD), f32)
        for n in range(QSTEPS):
            head, part = n // 2, n % 2
            rows = slice(part * QTILE, (part + 1) * QTILE)
            lanes = slice(head * HD, (head + 1) * HD)
            p = e_buf[n, at, :] * ratio[n : n + 1]
            ds = (p * (dp_buf[n, at, :] - delta[n : n + 1])).astype(bf16)
            ds_buf[n, at, :] = ds
            dv = dv + dot(p.astype(bf16), qd[1, rows, lanes], ((1,), (0,)))
            dk = dk + dot(ds, qd[0, rows, lanes], ((1,), (0,)))
        dk = dk * SCALE
        if k == 0:
            dkv_own[0] = dk[:SPAN]
            dkv_own[1] = dv[:SPAN]
            dkv_send[0, 1, 0] = dk[SPAN:].astype(bf16)
            dkv_send[0, 1, 1] = dv[SPAN:].astype(bf16)
            sent.append(
                send(
                    dkv_send.at[0, 1],
                    dkv_recv.at[1, 0],
                    dkv_send_sem.at[1, 0],
                    dkv_recv_sem.at[1, 0],
                    in_slab(partner),
                )
            )
        else:
            dkv_send[k, :, 0] = dk.astype(bf16).reshape(2, SPAN, HD)
            dkv_send[k, :, 1] = dv.astype(bf16).reshape(2, SPAN, HD)

            @pl.when(chunk - k >= 0)
            def _():
                dkv_copy(k, 0).start()

            @pl.when((chunk - k >= 0) & (apart != k))
            def _():
                dkv_copy(k, 1).start()

            @pl.when(apart == k)
            def _():
                dkv_recv[1, k] = dkv_send[k, 1]

    keys = kv[:, :, 0].reshape(2 * SPAN * WINDOW, HD)
    for n in range(QSTEPS):
        head, part = n // 2, n % 2
        dqt = dot(keys, ds_buf[n], ((0,), (0,)))
        dq_send[part * QTILE : (part + 1) * QTILE, head * HD : (head + 1) * HD] = (
            dqt.T * SCALE
        ).astype(bf16)
    for step in (4, 2, 6, 3, 5, 7, 1):
        to = (place + step) % 8
        sent.append(
            send(
                dq_send.at[rows_of(block_of(to, is_back))],
                dq_recv.at[is_back, shard],
                dq_send_sem.at[step],
                dq_recv_sem.at[is_back, shard],
                in_slab(to),
            )
        )
    dq_recv[is_back, shard] = dq_send[rows_of(own_block), :]

    def add_arrived(half, there, k, total):
        @pl.when(there & (apart != k) if half == 1 else there)
        def _():
            arrived(dkv_recv.at[half, k], dkv_recv_sem.at[half, k])

        @pl.when(there)
        def _():
            total[...] = total[...] + dkv_recv[half, k].astype(f32)

    for k in range(4, 0, -1):
        add_arrived(0, chunk + k < chunks, k, dkv_own)
    dk_out[own_rows, :] = dkv_own[0].astype(bf16)
    dv_out[own_rows, :] = dkv_own[1].astype(bf16)
    arrived(dkv_recv.at[1, 0], dkv_recv_sem.at[1, 0])
    dkv_own[...] = dkv_recv[1, 0].astype(f32)
    for k in range(4, 0, -1):
        add_arrived(1, other_chunk + k < chunks, k, dkv_own)
    dk_out[other_rows, :] = dkv_own[0].astype(bf16)
    dv_out[other_rows, :] = dkv_own[1].astype(bf16)

    for step in range(1, 8):
        source = (place + step) % 8
        source_x = source // 2
        source_back = source_x // 2
        source_unit = jnp.where(source_back == 1, 3 - source_x, source_x)
        source_shard = 2 * source_unit + source % 2
        arrived(
            dq_recv.at[source_back, source_shard], dq_recv_sem.at[source_back, source_shard]
        )
    for back in range(2):
        total_dq = dq_recv[back, 0].astype(f32)
        for j in range(1, 4):
            total_dq = total_dq + dq_recv[back, j].astype(f32)
        dq_out[back * SPAN : (back + 1) * SPAN, :] = total_dq.astype(bf16)

    for copy in sent:
        copy.wait_send()
    for k in range(1, WINDOW):

        @pl.when(chunk + k < chunks)
        def _():
            for half in range(2):
                kv_copy(k, half).wait_send()

        @pl.when(chunk - k >= 0)
        def _():
            dkv_copy(k, 0).wait_send()

        @pl.when((chunk - k >= 0) & (apart != k))
        def _():
            dkv_copy(k, 1).wait_send()


def write_out(dq, dk, dv, dq_out, dk_out, dv_out, sems):
    copies = [
        pltpu.make_async_copy(src, dst, sems.at[i])
        for i, (src, dst) in enumerate(((dq, dq_out), (dk, dk_out), (dv, dv_out)))
    ]
    for copy in copies:
        copy.start()
    for copy in copies:
        copy.wait()


def local(queries, key_rows, value_rows, grad_output, segments):
    groups = lax.axis_size("outer")
    slabs_per_group = lax.axis_size("inner") // 8
    slabs = groups * slabs_per_group
    rows = queries.shape[0]
    positions = segments.shape[0]
    vmem = pltpu.VMEM
    sem = pltpu.SemaphoreType.DMA
    keys = 2 * SPAN * WINDOW
    shapes = (
        jax.ShapeDtypeStruct((rows, HEADS * HD), bf16),
        jax.ShapeDtypeStruct((rows, HD), bf16),
        jax.ShapeDtypeStruct((rows, HD), bf16),
    )
    grads = pl.pallas_call(
        functools.partial(kernel, slabs_per_group, slabs, 32),
        out_shape=shapes,
        in_specs=[pl.BlockSpec(memory_space=pl.ANY)] * 5,
        out_specs=[pl.BlockSpec(memory_space=pltpu.VMEM)] * 3,
        scratch_shapes=[
            vmem((2, CHUNK, HEADS * HD), bf16),
            vmem((2, SPAN, HEADS * HD), bf16),
            vmem((WINDOW, 2, 2, SPAN, HD), bf16),
            vmem((2, SPAN, HD), bf16),
            vmem((positions // 128, 128), jnp.int32),
            vmem((CHUNK // QTILE, keys, QTILE), f32),
            vmem((QSTEPS, keys, QTILE), f32),
            vmem((QSTEPS, keys, QTILE), f32),
            vmem((QSTEPS, keys, QTILE), bf16),
            vmem((4, 3, 8, QTILE), f32),
            vmem((CHUNK, HEADS * HD), bf16),
            vmem((2, 4, SPAN, HEADS * HD), bf16),
            vmem((2, SPAN, HD), f32),
            vmem((WINDOW, 2, 2, SPAN, HD), bf16),
            vmem((2, WINDOW, 2, SPAN, HD), bf16),
            sem((8,)),
            sem,
            sem((7,)),
            sem((8,)),
            sem,
            sem,
            sem((WINDOW, 2)),
            sem((WINDOW, 2)),
            sem((3,)),
            sem((4,)),
            sem((8,)),
            sem((2, 4)),
            sem((2, WINDOW)),
            sem((2, WINDOW)),
        ],
        compiler_params=pltpu.CompilerParams(
            collective_id=0, has_side_effects=True, vmem_limit_bytes=60 * 1024 * 1024
        ),
        name="windowed_backward",
    )(queries, key_rows, value_rows, grad_output, segments.reshape(positions // 128, 128))
    return pl.pallas_call(
        write_out,
        out_shape=shapes,
        in_specs=[pl.BlockSpec(memory_space=pltpu.VMEM)] * 3,
        out_specs=[pl.BlockSpec(memory_space=pl.ANY)] * 3,
        scratch_shapes=[sem((3,))],
        name="write_out",
    )(*grads)


def solution(mesh):
    placed = P(("outer", "inner"), None)
    return jax.shard_map(
        local,
        mesh=mesh,
        in_specs=(placed, placed, placed, placed, P()),
        out_specs=(placed, placed, placed),
        check_vma=False,
    )
```

```python
import functools
import math

import jax
import jax.numpy as jnp
from jax import lax
from jax.experimental import pallas as pl
from jax.experimental.pallas import tpu as pltpu
from jax.sharding import PartitionSpec as P

MESH = pl.DeviceIdType.MESH
NEGATIVE = -1e30
TINY = 1e-30
HD = 128
HEADS = 3
SPAN = 64
CHUNK = 512
STRAIGHT = ()
WINDOW = 5
QTILE = 256
QSTEPS = HEADS * (CHUNK // QTILE)
SCALE = HD**-0.5
KAPPA = SCALE * math.log2(math.e)
f32 = jnp.float32
bf16 = jnp.bfloat16


def dot(a, b, dims):
    return lax.dot_general(a, b, ((dims[0], dims[1]), ((), ())), preferred_element_type=f32)


def kernel(
    slabs_per_group,
    slabs,
    docs,
    q_hbm,
    k_hbm,
    v_hbm,
    g_hbm,
    seg_hbm,
    dq_out,
    dk_out,
    dv_out,
    qd,
    qd_other,
    kv,
    kv_other,
    seg,
    bias,
    e_buf,
    dp_buf,
    ds_buf,
    stat,
    dq_send,
    dq_recv,
    dkv_own,
    dkv_send,
    dkv_recv,
    local_sem,
    seg_sem,
    qd_send_sem,
    qd_recv_sem,
    swap_send_sem,
    swap_recv_sem,
    kv_send_sem,
    kv_recv_sem,
    stat_send_sem,
    stat_recv_sem,
    dq_send_sem,
    dq_recv_sem,
    dkv_send_sem,
    dkv_recv_sem,
):
    chunks = 2 * slabs
    sent = []
    group = lax.axis_index("outer")
    inner = lax.axis_index("inner")
    place = inner % 8
    base = inner - place
    slab = group * slabs_per_group + inner // 8
    x = place // 2
    core = place % 2
    is_back = x // 2
    unit = jnp.where(is_back == 1, 3 - x, x)
    chunk = jnp.where(is_back == 1, chunks - 1 - slab, slab)
    other_chunk = chunks - 1 - chunk

    def in_slab(place_to):
        return (group, base + place_to)

    def holder(chunk_to, half=0):
        back = chunk_to // slabs
        slab_to = jnp.where(back == 1, chunks - 1 - chunk_to, chunk_to)
        x_to = jnp.where((back + half) % 2 == 1, 3 - unit, unit)
        return (
            slab_to // slabs_per_group,
            (slab_to % slabs_per_group) * 8 + x_to * 2 + core,
        )

    def block_of(place_of, back):
        return jnp.where(back == 1, 7 - place_of, place_of)

    def rows_of(block):
        return pl.ds(pl.multiple_of(block * SPAN, SPAN), SPAN)

    sibling = place + 1 - 2 * core
    partner = (3 - x) * 2 + core
    mate = (x + 1 - 2 * (x % 2)) * 2 + core
    far = (3 - (x + 1 - 2 * (x % 2))) * 2 + core
    own_block = block_of(place, is_back)
    own_rows = pl.ds(pl.multiple_of(is_back * SPAN, SPAN), SPAN)
    other_rows = pl.ds(pl.multiple_of((1 - is_back) * SPAN, SPAN), SPAN)

    locals_ = [
        pltpu.make_async_copy(k_hbm.at[own_rows], kv.at[0, 0, 0], local_sem.at[0]),
        pltpu.make_async_copy(v_hbm.at[own_rows], kv.at[0, 0, 1], local_sem.at[1]),
        pltpu.make_async_copy(k_hbm.at[other_rows], kv_other.at[0], local_sem.at[2]),
        pltpu.make_async_copy(v_hbm.at[other_rows], kv_other.at[1], local_sem.at[3]),
        pltpu.make_async_copy(q_hbm.at[other_rows], qd_other.at[0], local_sem.at[4]),
        pltpu.make_async_copy(g_hbm.at[other_rows], qd_other.at[1], local_sem.at[5]),
        pltpu.make_async_copy(q_hbm.at[own_rows], qd.at[0, rows_of(own_block)], local_sem.at[6]),
        pltpu.make_async_copy(g_hbm.at[own_rows], qd.at[1, rows_of(own_block)], local_sem.at[7]),
    ]
    for copy in locals_:
        copy.start()
    seg_copy = pltpu.make_async_copy(seg_hbm, seg, seg_sem)
    seg_copy.start()

    barrier = pltpu.get_barrier_semaphore()
    for k in (2, 3, 1, 4):
        for to, there in ((chunk + k, chunk + k < chunks), (chunk - k, chunk - k >= 0)):

            @pl.when(there)
            def _():
                pl.semaphore_signal(barrier, inc=1, device_id=holder(to), device_id_type=MESH)

    for step in range(1, 8):
        pl.semaphore_signal(
            barrier, inc=1, device_id=in_slab((place + step) % 8), device_id_type=MESH
        )
    later = jnp.minimum(chunks - 1 - chunk, WINDOW - 1)
    earlier = jnp.minimum(chunk, WINDOW - 1)
    apart = chunk - other_chunk
    for copy in locals_:
        copy.wait()
    pl.semaphore_wait(barrier, 7 + later + earlier)

    def send(src, dst, send_sem, recv_sem, to):
        copy = pltpu.make_async_remote_copy(
            src_ref=src,
            dst_ref=dst,
            send_sem=send_sem,
            recv_sem=recv_sem,
            device_id=to,
            device_id_type=MESH,
        )
        copy.start()
        return copy

    def arrived(dst, recv_sem):
        pltpu.make_async_copy(dst, dst, recv_sem).wait()

    def qd_block(block):
        return qd.at[:, rows_of(block)]

    def send_block(src, block, sem, to):
        return send(src, qd_block(block), qd_send_sem.at[sem], qd_recv_sem.at[block], in_slab(to))

    sent.append(send(kv_other, kv.at[0, 1], swap_send_sem, swap_recv_sem, in_slab(partner)))

    def kv_copy(k, half):
        straight = half == 1 and k in STRAIGHT
        return pltpu.make_async_remote_copy(
            src_ref=kv_other if straight else kv.at[0, half],
            dst_ref=kv.at[k, half],
            send_sem=kv_send_sem.at[k, half],
            recv_sem=kv_recv_sem.at[k, half],
            device_id=holder((other_chunk if straight else chunk) + k),
            device_id_type=MESH,
        )

    def kv_sent(k, half):
        if half == 1 and k in STRAIGHT:
            return (other_chunk + k < chunks) & (apart != k)
        return chunk + k < chunks

    def kv_arrives(k, half):
        if half == 1 and k in STRAIGHT:
            return (chunk - k >= 0) & (apart != k)
        return chunk - k >= 0

    def kv_start(half, which):
        for k in which:

            @pl.when(kv_sent(k, half))
            def _():
                kv_copy(k, half).start()

    other_block = block_of(place, 1 - is_back)
    kv_start(1, STRAIGHT)
    kv_start(0, (2, 3, 1, 4))
    sent.append(send_block(qd_other, other_block, 0, far))
    sent.append(send_block(qd_block(own_block), own_block, 1, mate))
    sent.append(send_block(qd_other, other_block, 2, partner))
    sent.append(send_block(qd_block(own_block), own_block, 3, sibling))

    for k in range(1, WINDOW):

        @pl.when(chunk - k < 0)
        def _():
            kv[k] = jnp.zeros(kv.shape[1:], bf16)

        if k in STRAIGHT:

            @pl.when(apart == k)
            def _():
                kv[k, 1] = kv_other[...]

    seg_copy.wait()
    doc_ids = lax.broadcasted_iota(jnp.int32, (docs, 128), 0)

    def count(i, acc):
        rows = seg[pl.ds(pl.multiple_of(i * 8, 8), 8), :]
        for r in range(8):
            acc = acc + jnp.where(rows[r : r + 1, :] < doc_ids, 1.0, 0.0)
        return acc

    tally = lax.fori_loop(0, seg.shape[0] // 8, count, jnp.zeros((docs, 128), f32))
    firsts = jnp.sum(tally, axis=1, keepdims=True)
    query_pos = (lax.broadcasted_iota(jnp.int32, (1, CHUNK), 1) + chunk * CHUNK).astype(f32)
    starts = jnp.max(jnp.where(firsts <= query_pos, firsts, 0.0), axis=0, keepdims=True)
    row_ids = lax.broadcasted_iota(jnp.int32, (SPAN, QTILE), 0)
    for k in range(WINDOW):
        key_chunk = chunk - k
        back = (key_chunk + slabs) // slabs - 1
        for half in range(2):
            front_place = jnp.where(half == 0, unit, 3 - unit) * 2 + core
            back_place = jnp.where(half == 0, 3 - unit, unit) * 2 + core
            block = jnp.where(back == 1, 7 - back_place, front_place)
            key_pos = (row_ids + (key_chunk * CHUNK + block * SPAN)).astype(f32)
            for part in range(CHUNK // QTILE):
                lanes = slice(part * QTILE, (part + 1) * QTILE)
                allowed = (key_pos >= starts[:, lanes]) & (key_pos <= query_pos[:, lanes])
                at = (2 * k + half) * SPAN
                bias[part, at : at + SPAN, :] = jnp.where(allowed, 0.0, NEGATIVE)

    arrived(kv.at[0, 1], swap_recv_sem)
    kv_start(1, [k for k in (2, 3, 1, 4) if k not in STRAIGHT])
    for sem, source in ((4, mate), (5, partner), (6, far)):
        block = block_of(source, is_back)
        arrived(qd_block(block), qd_recv_sem.at[block])
        sent.append(send_block(qd_block(block), block, sem, sibling))
    for step in range(4):
        block = block_of((sibling + 2 * step) % 8, is_back)
        arrived(qd_block(block), qd_recv_sem.at[block])
    for k in range(1, WINDOW):

        for half in range(2):

            @pl.when(kv_arrives(k, half))
            def _():
                arrived(kv.at[k, half], kv_recv_sem.at[k, half])

    def tile(n):
        head = n // 2
        part = n % 2
        return (
            part,
            pl.ds(pl.multiple_of(part * QTILE, QTILE), QTILE),
            pl.ds(pl.multiple_of(head * HD, HD), HD),
        )

    def keys_of(k):
        return kv[k, :, 0].reshape(2 * SPAN, HD)

    def values_of(k):
        return kv[k, :, 1].reshape(2 * SPAN, HD)

    shard = 2 * unit + core
    def forward(n, carry):
        part, rows, lanes = tile(n)
        q = qd[0, rows, lanes]
        g = qd[1, rows, lanes]
        top = jnp.full((1, QTILE), NEGATIVE, f32)
        for k in range(WINDOW):
            at = slice(2 * SPAN * k, 2 * SPAN * (k + 1))
            s = dot(keys_of(k), q, ((1,), (1,))) + bias[part, at, :]
            e_buf[n, at, :] = s
            top = jnp.maximum(top, jnp.max(s, axis=0, keepdims=True))
        total = jnp.zeros((1, QTILE), f32)
        slope = jnp.zeros((1, QTILE), f32)
        for k in range(WINDOW):
            at = slice(2 * SPAN * k, 2 * SPAN * (k + 1))
            dp = dot(values_of(k), g, ((1,), (1,)))
            e = jnp.exp2((e_buf[n, at, :] - top) * KAPPA)
            e_buf[n, at, :] = e
            dp_buf[n, at, :] = dp
            total = total + jnp.sum(e, axis=0, keepdims=True)
            slope = slope + jnp.sum(e * dp, axis=0, keepdims=True)
        stat[shard, 0, pl.ds(n, 1), :] = top
        stat[shard, 1, pl.ds(n, 1), :] = total
        stat[shard, 2, pl.ds(n, 1), :] = slope
        return carry

    stat[shard] = jnp.zeros(stat.shape[1:], f32)
    lax.fori_loop(0, QSTEPS, forward, 0)
    for sem, to in ((0, mate), (1, sibling), (2, mate + 1 - 2 * core)):
        sent.append(
            send(
                stat.at[shard],
                stat.at[shard],
                stat_send_sem.at[sem],
                stat_recv_sem.at[shard],
                in_slab(to),
            )
        )
    for step in range(1, 4):
        peer = (shard + step) % 4
        arrived(stat.at[peer], stat_recv_sem.at[peer])
    tops = stat[:, 0]
    top = jnp.max(tops, axis=0)
    factors = jnp.exp2((tops - top[None]) * KAPPA)
    inverse = 1.0 / jnp.maximum(jnp.sum(stat[:, 1] * factors, axis=0), TINY)
    delta = jnp.sum(stat[:, 2] * factors, axis=0) * inverse
    ratio = jnp.exp2((stat[shard, 0] - top) * KAPPA) * inverse
    def dkv_copy(k, half):
        return pltpu.make_async_remote_copy(
            src_ref=dkv_send.at[k, half],
            dst_ref=dkv_recv.at[half, k],
            send_sem=dkv_send_sem.at[half, k],
            recv_sem=dkv_recv_sem.at[half, k],
            device_id=holder(chunk - k, half),
            device_id_type=MESH,
        )
    for k in (2, 3, 1, 4, 0):
        at = slice(2 * SPAN * k, 2 * SPAN * (k + 1))
        dk = jnp.zeros((2 * SPAN, HD), f32)
        dv = jnp.zeros((2 * SPAN, HD), f32)
        for n in range(QSTEPS):
            head, part = n // 2, n % 2
            rows = slice(part * QTILE, (part + 1) * QTILE)
            lanes = slice(head * HD, (head + 1) * HD)
            p = e_buf[n, at, :] * ratio[n : n + 1]
            ds = (p * (dp_buf[n, at, :] - delta[n : n + 1])).astype(bf16)
            ds_buf[n, at, :] = ds
            dv = dv + dot(p.astype(bf16), qd[1, rows, lanes], ((1,), (0,)))
            dk = dk + dot(ds, qd[0, rows, lanes], ((1,), (0,)))
        dk = dk * SCALE
        if k == 0:
            dkv_own[0] = dk[:SPAN]
            dkv_own[1] = dv[:SPAN]
            dkv_send[0, 1, 0] = dk[SPAN:].astype(bf16)
            dkv_send[0, 1, 1] = dv[SPAN:].astype(bf16)
            sent.append(
                send(
                    dkv_send.at[0, 1],
                    dkv_recv.at[1, 0],
                    dkv_send_sem.at[1, 0],
                    dkv_recv_sem.at[1, 0],
                    in_slab(partner),
                )
            )
        else:
            dkv_send[k, :, 0] = dk.astype(bf16).reshape(2, SPAN, HD)
            dkv_send[k, :, 1] = dv.astype(bf16).reshape(2, SPAN, HD)

            @pl.when(chunk - k >= 0)
            def _():
                dkv_copy(k, 0).start()

            @pl.when((chunk - k >= 0) & (apart != k))
            def _():
                dkv_copy(k, 1).start()

            @pl.when(apart == k)
            def _():
                dkv_recv[1, k] = dkv_send[k, 1]
    keys = kv[:, :, 0].reshape(2 * SPAN * WINDOW, HD)
    for n in range(QSTEPS):
        head, part = n // 2, n % 2
        dqt = dot(keys, ds_buf[n], ((0,), (0,)))
        dq_send[part * QTILE : (part + 1) * QTILE, head * HD : (head + 1) * HD] = (
            dqt.T * SCALE
        ).astype(bf16)
    for step in (4, 2, 6, 3, 5, 7, 1):
        to = (place + step) % 8
        sent.append(
            send(
                dq_send.at[rows_of(block_of(to, is_back))],
                dq_recv.at[is_back, shard],
                dq_send_sem.at[step],
                dq_recv_sem.at[is_back, shard],
                in_slab(to),
            )
        )
    dq_recv[is_back, shard] = dq_send[rows_of(own_block), :]
    def add_arrived(half, there, k, total):
        @pl.when(there & (apart != k) if half == 1 else there)
        def _():
            arrived(dkv_recv.at[half, k], dkv_recv_sem.at[half, k])

        @pl.when(there)
        def _():
            total[...] = total[...] + dkv_recv[half, k].astype(f32)

    for k in range(4, 0, -1):
        add_arrived(0, chunk + k < chunks, k, dkv_own)
    dk_out[own_rows, :] = dkv_own[0].astype(bf16)
    dv_out[own_rows, :] = dkv_own[1].astype(bf16)
    arrived(dkv_recv.at[1, 0], dkv_recv_sem.at[1, 0])
    dkv_own[...] = dkv_recv[1, 0].astype(f32)
    for k in range(4, 0, -1):
        add_arrived(1, other_chunk + k < chunks, k, dkv_own)
    dk_out[other_rows, :] = dkv_own[0].astype(bf16)
    dv_out[other_rows, :] = dkv_own[1].astype(bf16)
    for step in range(1, 8):
        source = (place + step) % 8
        source_x = source // 2
        source_back = source_x // 2
        source_unit = jnp.where(source_back == 1, 3 - source_x, source_x)
        source_shard = 2 * source_unit + source % 2
        arrived(
            dq_recv.at[source_back, source_shard], dq_recv_sem.at[source_back, source_shard]
        )
    for back in range(2):
        total_dq = dq_recv[back, 0].astype(f32)
        for j in range(1, 4):
            total_dq = total_dq + dq_recv[back, j].astype(f32)
        dq_out[back * SPAN : (back + 1) * SPAN, :] = total_dq.astype(bf16)
    for copy in sent:
        copy.wait_send()
    for k in range(1, WINDOW):

        for half in range(2):

            @pl.when(kv_sent(k, half))
            def _():
                kv_copy(k, half).wait_send()
    for k in range(1, WINDOW):

        @pl.when(chunk - k >= 0)
        def _():
            dkv_copy(k, 0).wait_send()

        @pl.when((chunk - k >= 0) & (apart != k))
        def _():
            dkv_copy(k, 1).wait_send()


def write_out(dq, dk, dv, dq_out, dk_out, dv_out, sems):
    copies = [
        pltpu.make_async_copy(src, dst, sems.at[i])
        for i, (src, dst) in enumerate(((dq, dq_out), (dk, dk_out), (dv, dv_out)))
    ]
    for copy in copies:
        copy.start()
    for copy in copies:
        copy.wait()


def local(queries, key_rows, value_rows, grad_output, segments):
    groups = lax.axis_size("outer")
    slabs_per_group = lax.axis_size("inner") // 8
    slabs = groups * slabs_per_group
    rows = queries.shape[0]
    positions = segments.shape[0]
    vmem = pltpu.VMEM
    sem = pltpu.SemaphoreType.DMA
    keys = 2 * SPAN * WINDOW
    shapes = (
        jax.ShapeDtypeStruct((rows, HEADS * HD), bf16),
        jax.ShapeDtypeStruct((rows, HD), bf16),
        jax.ShapeDtypeStruct((rows, HD), bf16),
    )
    grads = pl.pallas_call(
        functools.partial(kernel, slabs_per_group, slabs, 32),
        out_shape=shapes,
        in_specs=[pl.BlockSpec(memory_space=pl.ANY)] * 5,
        out_specs=[pl.BlockSpec(memory_space=pltpu.VMEM)] * 3,
        scratch_shapes=[
            vmem((2, CHUNK, HEADS * HD), bf16),
            vmem((2, SPAN, HEADS * HD), bf16),
            vmem((WINDOW, 2, 2, SPAN, HD), bf16),
            vmem((2, SPAN, HD), bf16),
            vmem((positions // 128, 128), jnp.int32),
            vmem((CHUNK // QTILE, keys, QTILE), f32),
            vmem((QSTEPS, keys, QTILE), f32),
            vmem((QSTEPS, keys, QTILE), f32),
            vmem((QSTEPS, keys, QTILE), bf16),
            vmem((4, 3, 8, QTILE), f32),
            vmem((CHUNK, HEADS * HD), bf16),
            vmem((2, 4, SPAN, HEADS * HD), bf16),
            vmem((2, SPAN, HD), f32),
            vmem((WINDOW, 2, 2, SPAN, HD), bf16),
            vmem((2, WINDOW, 2, SPAN, HD), bf16),
            sem((8,)),
            sem,
            sem((7,)),
            sem((8,)),
            sem,
            sem,
            sem((WINDOW, 2)),
            sem((WINDOW, 2)),
            sem((3,)),
            sem((4,)),
            sem((8,)),
            sem((2, 4)),
            sem((2, WINDOW)),
            sem((2, WINDOW)),
        ],
        compiler_params=pltpu.CompilerParams(
            collective_id=0, has_side_effects=True, vmem_limit_bytes=60 * 1024 * 1024
        ),
        name="windowed_backward",
    )(queries, key_rows, value_rows, grad_output, segments.reshape(positions // 128, 128))
    return pl.pallas_call(
        write_out,
        out_shape=shapes,
        in_specs=[pl.BlockSpec(memory_space=pltpu.VMEM)] * 3,
        out_specs=[pl.BlockSpec(memory_space=pl.ANY)] * 3,
        scratch_shapes=[sem((3,))],
        name="write_out",
    )(*grads)


def solution(mesh):
    placed = P(("outer", "inner"), None)
    return jax.shard_map(
        local,
        mesh=mesh,
        in_specs=(placed, placed, placed, placed, P()),
        out_specs=(placed, placed, placed),
        check_vma=False,
    )
```

```python
import functools
import math

import jax
import jax.numpy as jnp
from jax import lax
from jax.experimental import pallas as pl
from jax.experimental.pallas import tpu as pltpu
from jax.sharding import PartitionSpec as P

MESH = pl.DeviceIdType.MESH
NEGATIVE = -1e30
TINY = 1e-30
HD = 128
HEADS = 3
SPAN = 64
CHUNK = 512
WINDOW = 5
QTILE = 256
QSTEPS = HEADS * (CHUNK // QTILE)
SCALE = HD**-0.5
KAPPA = SCALE * math.log2(math.e)
f32 = jnp.float32
bf16 = jnp.bfloat16


def dot(a, b, dims):
    return lax.dot_general(a, b, ((dims[0], dims[1]), ((), ())), preferred_element_type=f32)


def kernel(
    slabs_per_group,
    slabs,
    docs,
    q_hbm,
    k_hbm,
    v_hbm,
    g_hbm,
    seg_hbm,
    dq_out,
    dk_out,
    dv_out,
    qd,
    qd_other,
    kv,
    kv_other,
    seg,
    bias,
    half_stat,
    e_buf,
    dp_buf,
    ds_buf,
    stat,
    dq_send,
    dq_recv,
    dkv_own,
    dkv_send,
    dkv_recv,
    near_sem,
    far_sem,
    local_sem,
    seg_sem,
    qd_send_sem,
    qd_recv_sem,
    swap_send_sem,
    swap_recv_sem,
    kv_send_sem,
    kv_recv_sem,
    stat_send_sem,
    stat_recv_sem,
    dq_send_sem,
    dq_recv_sem,
    dkv_send_sem,
    dkv_recv_sem,
):
    chunks = 2 * slabs
    sent = []
    group = lax.axis_index("outer")
    inner = lax.axis_index("inner")
    place = inner % 8
    base = inner - place
    slab = group * slabs_per_group + inner // 8
    x = place // 2
    core = place % 2
    is_back = x // 2
    unit = jnp.where(is_back == 1, 3 - x, x)
    chunk = jnp.where(is_back == 1, chunks - 1 - slab, slab)
    other_chunk = chunks - 1 - chunk

    def in_slab(place_to):
        return (group, base + place_to)

    def holder(chunk_to, half=0, core_to=core):
        back = chunk_to // slabs
        slab_to = jnp.where(back == 1, chunks - 1 - chunk_to, chunk_to)
        x_to = jnp.where((back + half) % 2 == 1, 3 - unit, unit)
        return (
            slab_to // slabs_per_group,
            (slab_to % slabs_per_group) * 8 + x_to * 2 + core_to,
        )

    def block_of(place_of, back):
        return jnp.where(back == 1, 7 - place_of, place_of)

    def rows_of(block):
        return pl.ds(pl.multiple_of(block * SPAN, SPAN), SPAN)

    sibling = place + 1 - 2 * core
    partner = (3 - x) * 2 + core
    mate = (x + 1 - 2 * (x % 2)) * 2 + core
    far = (3 - (x + 1 - 2 * (x % 2))) * 2 + core
    own_block = block_of(place, is_back)
    own_rows = pl.ds(pl.multiple_of(is_back * SPAN, SPAN), SPAN)
    other_rows = pl.ds(pl.multiple_of((1 - is_back) * SPAN, SPAN), SPAN)

    locals_ = [
        pltpu.make_async_copy(k_hbm.at[own_rows], kv.at[0, 0, 0], local_sem.at[0]),
        pltpu.make_async_copy(v_hbm.at[own_rows], kv.at[0, 0, 1], local_sem.at[1]),
        pltpu.make_async_copy(k_hbm.at[other_rows], kv_other.at[0], local_sem.at[2]),
        pltpu.make_async_copy(v_hbm.at[other_rows], kv_other.at[1], local_sem.at[3]),
        pltpu.make_async_copy(q_hbm.at[other_rows], qd_other.at[0], local_sem.at[4]),
        pltpu.make_async_copy(g_hbm.at[other_rows], qd_other.at[1], local_sem.at[5]),
        pltpu.make_async_copy(q_hbm.at[own_rows], qd.at[0, rows_of(own_block)], local_sem.at[6]),
        pltpu.make_async_copy(g_hbm.at[own_rows], qd.at[1, rows_of(own_block)], local_sem.at[7]),
    ]
    for copy in locals_:
        copy.start()
    seg_copy = pltpu.make_async_copy(seg_hbm, seg, seg_sem)
    seg_copy.start()

    barrier = pltpu.get_barrier_semaphore()
    for k in (2, 3, 1, 4):

        @pl.when(chunk - k >= 0)
        def _():
            pl.semaphore_signal(
                barrier, inc=1, device_id=holder(chunk - k, 0, 1), device_id_type=MESH
            )

    for step in range(4):
        to_x = (x + step) % 4

        @pl.when((step > 0) | (core == 1))
        def _():
            pl.semaphore_signal(barrier, inc=1, device_id=in_slab(2 * to_x), device_id_type=MESH)

    later = jnp.minimum(chunks - 1 - chunk, WINDOW - 1)
    apart = chunk - other_chunk

    @pl.when(core == 0)
    def _():
        pl.semaphore_wait(barrier, 7)
        pl.semaphore_signal(near_sem, inc=1, device_id=in_slab(sibling), device_id_type=MESH)

    @pl.when(core == 1)
    def _():
        pl.semaphore_wait(near_sem, 1)

    for copy in locals_:
        copy.wait()

    def send(src, dst, send_sem, recv_sem, to):
        copy = pltpu.make_async_remote_copy(
            src_ref=src,
            dst_ref=dst,
            send_sem=send_sem,
            recv_sem=recv_sem,
            device_id=to,
            device_id_type=MESH,
        )
        copy.start()
        return copy

    def arrived(dst, recv_sem):
        pltpu.make_async_copy(dst, dst, recv_sem).wait()

    def qd_block(block):
        return qd.at[:, rows_of(block)]

    def send_block(src, block, sem, to):
        return send(src, qd_block(block), qd_send_sem.at[sem], qd_recv_sem.at[block], in_slab(to))

    sent.append(send(kv_other, kv.at[1, 0], swap_send_sem, swap_recv_sem, in_slab(partner)))

    def kv_copy(k, half):
        return pltpu.make_async_remote_copy(
            src_ref=kv.at[half, 0],
            dst_ref=kv.at[half, k],
            send_sem=kv_send_sem.at[half, k],
            recv_sem=kv_recv_sem.at[half, k],
            device_id=holder(chunk + k),
            device_id_type=MESH,
        )

    def kv_start(half):
        for k in (2, 3, 1, 4):

            @pl.when(chunk + k < chunks)
            def _():
                kv_copy(k, half).start()

    other_block = block_of(place, 1 - is_back)
    sent.append(send_block(qd_other, other_block, 0, far))
    sent.append(send_block(qd_block(own_block), own_block, 1, mate))
    sent.append(send_block(qd_other, other_block, 2, partner))
    sent.append(send_block(qd_block(own_block), own_block, 3, sibling))

    @pl.when(core == 1)
    def _():
        @pl.when(later > 0)
        def _():
            pl.semaphore_wait(barrier, 2 * later)

        pl.semaphore_signal(far_sem, inc=1, device_id=in_slab(sibling), device_id_type=MESH)

    @pl.when(core == 0)
    def _():
        pl.semaphore_wait(far_sem, 1)

    kv_start(0)
    arrived(kv.at[1, 0], swap_recv_sem)
    kv_start(1)

    for k in range(1, WINDOW):

        @pl.when(chunk - k < 0)
        def _():
            kv[:, k] = jnp.zeros((2,) + kv.shape[2:], bf16)

    seg_copy.wait()
    doc_ids = lax.broadcasted_iota(jnp.int32, (docs, 128), 0)

    def count(i, acc):
        rows = seg[pl.ds(pl.multiple_of(i * 8, 8), 8), :]
        for r in range(8):
            acc = acc + jnp.where(rows[r : r + 1, :] < doc_ids, 1.0, 0.0)
        return acc

    tally = lax.fori_loop(0, seg.shape[0] // 8, count, jnp.zeros((docs, 128), f32))
    firsts = jnp.sum(tally, axis=1, keepdims=True)
    query_pos = (lax.broadcasted_iota(jnp.int32, (1, CHUNK), 1) + chunk * CHUNK).astype(f32)
    starts = jnp.max(jnp.where(firsts <= query_pos, firsts, 0.0), axis=0, keepdims=True)
    row_ids = lax.broadcasted_iota(jnp.int32, (SPAN, QTILE), 0)
    for k in range(WINDOW):
        key_chunk = chunk - k
        back = (key_chunk + slabs) // slabs - 1
        for half in range(2):
            front_place = jnp.where(half == 0, unit, 3 - unit) * 2 + core
            back_place = jnp.where(half == 0, 3 - unit, unit) * 2 + core
            block = jnp.where(back == 1, 7 - back_place, front_place)
            key_pos = (row_ids + (key_chunk * CHUNK + block * SPAN)).astype(f32)
            for part in range(CHUNK // QTILE):
                lanes = slice(part * QTILE, (part + 1) * QTILE)
                allowed = (key_pos >= starts[:, lanes]) & (key_pos <= query_pos[:, lanes])
                at = (WINDOW * half + k) * SPAN
                bias[part, at : at + SPAN, :] = jnp.where(allowed, 0.0, NEGATIVE)

    for sem, source in ((4, mate), (5, partner), (6, far)):
        block = block_of(source, is_back)
        arrived(qd_block(block), qd_recv_sem.at[block])
        sent.append(send_block(qd_block(block), block, sem, sibling))
    for step in range(4):
        block = block_of((sibling + 2 * step) % 8, is_back)
        arrived(qd_block(block), qd_recv_sem.at[block])
    shard = 2 * unit + core

    def forward(half):
        at = slice(WINDOW * SPAN * half, WINDOW * SPAN * (half + 1))
        keys = kv[half, :, 0].reshape(WINDOW * SPAN, HD)
        values = kv[half, :, 1].reshape(WINDOW * SPAN, HD)
        for n in range(QSTEPS):
            head, part = n // 2, n % 2
            rows = slice(part * QTILE, (part + 1) * QTILE)
            lanes = slice(head * HD, (head + 1) * HD)
            s = dot(keys, qd[0, rows, lanes], ((1,), (1,))) + bias[part, at, :]
            dp = dot(values, qd[1, rows, lanes], ((1,), (1,)))
            top = jnp.max(s, axis=0, keepdims=True)
            e = jnp.exp2((s - top) * KAPPA)
            e_buf[n, at, :] = e
            dp_buf[n, at, :] = dp
            half_stat[half, 0, n : n + 1, :] = top
            half_stat[half, 1, n : n + 1, :] = jnp.sum(e, axis=0, keepdims=True)
            half_stat[half, 2, n : n + 1, :] = jnp.sum(e * dp, axis=0, keepdims=True)

    half_stat[...] = jnp.zeros(half_stat.shape, f32)
    for half in range(2):
        for k in range(1, WINDOW):

            @pl.when(chunk - k >= 0)
            def _():
                arrived(kv.at[half, k], kv_recv_sem.at[half, k])
        forward(half)
    def combined(parts):
        top = jnp.max(parts[:, 0], axis=0)
        factors = jnp.exp2((parts[:, 0] - top[None]) * KAPPA)
        return (
            top,
            jnp.sum(parts[:, 1] * factors, axis=0),
            jnp.sum(parts[:, 2] * factors, axis=0),
        )

    for i, row in enumerate(combined(half_stat[...])):
        stat[shard, i] = row
    for sem, to in ((0, mate), (1, sibling), (2, mate + 1 - 2 * core)):
        sent.append(
            send(
                stat.at[shard],
                stat.at[shard],
                stat_send_sem.at[sem],
                stat_recv_sem.at[shard],
                in_slab(to),
            )
        )
    for step in range(1, 4):
        peer = (shard + step) % 4
        arrived(stat.at[peer], stat_recv_sem.at[peer])
    top, total, slope = combined(stat[...])
    inverse = 1.0 / jnp.maximum(total, TINY)
    delta = slope * inverse
    ratios = [jnp.exp2((half_stat[half, 0] - top) * KAPPA) * inverse for half in range(2)]

    def dkv_copy(k, half):
        return pltpu.make_async_remote_copy(
            src_ref=dkv_send.at[k, half],
            dst_ref=dkv_recv.at[half, k],
            send_sem=dkv_send_sem.at[half, k],
            recv_sem=dkv_recv_sem.at[half, k],
            device_id=holder(chunk - k, half),
            device_id_type=MESH,
        )
    for k in (2, 3, 1, 4, 0):
        dk = jnp.zeros((2 * SPAN, HD), f32)
        dv = jnp.zeros((2 * SPAN, HD), f32)
        for n in range(QSTEPS):
            head, part = n // 2, n % 2
            rows = slice(part * QTILE, (part + 1) * QTILE)
            lanes = slice(head * HD, (head + 1) * HD)
            p_halves, ds_halves = [], []
            for half in range(2):
                at = slice((WINDOW * half + k) * SPAN, (WINDOW * half + k + 1) * SPAN)
                p = e_buf[n, at, :] * ratios[half][n : n + 1]
                ds = (p * (dp_buf[n, at, :] - delta[n : n + 1])).astype(bf16)
                ds_buf[n, at, :] = ds
                p_halves.append(p.astype(bf16))
                ds_halves.append(ds)
            p = jnp.concatenate(p_halves, axis=0)
            ds = jnp.concatenate(ds_halves, axis=0)
            dv = dv + dot(p, qd[1, rows, lanes], ((1,), (0,)))
            dk = dk + dot(ds, qd[0, rows, lanes], ((1,), (0,)))
        dk = dk * SCALE
        if k == 0:
            dkv_own[0] = dk[:SPAN]
            dkv_own[1] = dv[:SPAN]
            dkv_send[0, 1, 0] = dk[SPAN:].astype(bf16)
            dkv_send[0, 1, 1] = dv[SPAN:].astype(bf16)
            sent.append(
                send(
                    dkv_send.at[0, 1],
                    dkv_recv.at[1, 0],
                    dkv_send_sem.at[1, 0],
                    dkv_recv_sem.at[1, 0],
                    in_slab(partner),
                )
            )
        else:
            dkv_send[k, :, 0] = dk.astype(bf16).reshape(2, SPAN, HD)
            dkv_send[k, :, 1] = dv.astype(bf16).reshape(2, SPAN, HD)

            @pl.when(chunk - k >= 0)
            def _():
                dkv_copy(k, 0).start()

            @pl.when((chunk - k >= 0) & (apart != k))
            def _():
                dkv_copy(k, 1).start()

            @pl.when(apart == k)
            def _():
                dkv_recv[1, k] = dkv_send[k, 1]
    keys = kv[:, :, 0].reshape(2 * SPAN * WINDOW, HD)
    for n in range(QSTEPS):
        head, part = n // 2, n % 2
        dqt = dot(keys, ds_buf[n], ((0,), (0,)))
        dq_send[part * QTILE : (part + 1) * QTILE, head * HD : (head + 1) * HD] = (
            dqt.T * SCALE
        ).astype(bf16)
    for step in (4, 2, 6, 3, 5, 7, 1):
        to = (place + step) % 8
        sent.append(
            send(
                dq_send.at[rows_of(block_of(to, is_back))],
                dq_recv.at[is_back, shard],
                dq_send_sem.at[step],
                dq_recv_sem.at[is_back, shard],
                in_slab(to),
            )
        )
    dq_recv[is_back, shard] = dq_send[rows_of(own_block), :]
    def add_arrived(half, there, k, total):
        @pl.when(there & (apart != k) if half == 1 else there)
        def _():
            arrived(dkv_recv.at[half, k], dkv_recv_sem.at[half, k])

        @pl.when(there)
        def _():
            total[...] = total[...] + dkv_recv[half, k].astype(f32)

    for k in range(4, 0, -1):
        add_arrived(0, chunk + k < chunks, k, dkv_own)
    dk_out[own_rows, :] = dkv_own[0].astype(bf16)
    dv_out[own_rows, :] = dkv_own[1].astype(bf16)
    arrived(dkv_recv.at[1, 0], dkv_recv_sem.at[1, 0])
    dkv_own[...] = dkv_recv[1, 0].astype(f32)
    for k in range(4, 0, -1):
        add_arrived(1, other_chunk + k < chunks, k, dkv_own)
    dk_out[other_rows, :] = dkv_own[0].astype(bf16)
    dv_out[other_rows, :] = dkv_own[1].astype(bf16)
    for step in range(1, 8):
        source = (place + step) % 8
        source_x = source // 2
        source_back = source_x // 2
        source_unit = jnp.where(source_back == 1, 3 - source_x, source_x)
        source_shard = 2 * source_unit + source % 2
        arrived(
            dq_recv.at[source_back, source_shard], dq_recv_sem.at[source_back, source_shard]
        )
    for back in range(2):
        total_dq = dq_recv[back, 0].astype(f32)
        for j in range(1, 4):
            total_dq = total_dq + dq_recv[back, j].astype(f32)
        dq_out[back * SPAN : (back + 1) * SPAN, :] = total_dq.astype(bf16)
    for copy in sent:
        copy.wait_send()
    for k in range(1, WINDOW):

        @pl.when(chunk + k < chunks)
        def _():
            for half in range(2):
                kv_copy(k, half).wait_send()
    for k in range(1, WINDOW):

        @pl.when(chunk - k >= 0)
        def _():
            dkv_copy(k, 0).wait_send()

        @pl.when((chunk - k >= 0) & (apart != k))
        def _():
            dkv_copy(k, 1).wait_send()


def write_out(dq, dk, dv, dq_out, dk_out, dv_out, sems):
    copies = [
        pltpu.make_async_copy(src, dst, sems.at[i])
        for i, (src, dst) in enumerate(((dq, dq_out), (dk, dk_out), (dv, dv_out)))
    ]
    for copy in copies:
        copy.start()
    for copy in copies:
        copy.wait()


def local(queries, key_rows, value_rows, grad_output, segments):
    groups = lax.axis_size("outer")
    slabs_per_group = lax.axis_size("inner") // 8
    slabs = groups * slabs_per_group
    rows = queries.shape[0]
    positions = segments.shape[0]
    vmem = pltpu.VMEM
    sem = pltpu.SemaphoreType.DMA
    keys = 2 * SPAN * WINDOW
    shapes = (
        jax.ShapeDtypeStruct((rows, HEADS * HD), bf16),
        jax.ShapeDtypeStruct((rows, HD), bf16),
        jax.ShapeDtypeStruct((rows, HD), bf16),
    )
    grads = pl.pallas_call(
        functools.partial(kernel, slabs_per_group, slabs, 32),
        out_shape=shapes,
        in_specs=[pl.BlockSpec(memory_space=pl.ANY)] * 5,
        out_specs=[pl.BlockSpec(memory_space=pltpu.VMEM)] * 3,
        scratch_shapes=[
            vmem((2, CHUNK, HEADS * HD), bf16),
            vmem((2, SPAN, HEADS * HD), bf16),
            vmem((2, WINDOW, 2, SPAN, HD), bf16),
            vmem((2, SPAN, HD), bf16),
            vmem((positions // 128, 128), jnp.int32),
            vmem((CHUNK // QTILE, keys, QTILE), f32),
            vmem((2, 3, 8, QTILE), f32),
            vmem((QSTEPS, keys, QTILE), f32),
            vmem((QSTEPS, keys, QTILE), f32),
            vmem((QSTEPS, keys, QTILE), bf16),
            vmem((4, 3, 8, QTILE), f32),
            vmem((CHUNK, HEADS * HD), bf16),
            vmem((2, 4, SPAN, HEADS * HD), bf16),
            vmem((2, SPAN, HD), f32),
            vmem((WINDOW, 2, 2, SPAN, HD), bf16),
            vmem((2, WINDOW, 2, SPAN, HD), bf16),
            pltpu.SemaphoreType.REGULAR,
            pltpu.SemaphoreType.REGULAR,
            sem((8,)),
            sem,
            sem((7,)),
            sem((8,)),
            sem,
            sem,
            sem((2, WINDOW)),
            sem((2, WINDOW)),
            sem((3,)),
            sem((4,)),
            sem((8,)),
            sem((2, 4)),
            sem((2, WINDOW)),
            sem((2, WINDOW)),
        ],
        compiler_params=pltpu.CompilerParams(
            collective_id=0, has_side_effects=True, vmem_limit_bytes=60 * 1024 * 1024
        ),
        name="windowed_backward",
    )(queries, key_rows, value_rows, grad_output, segments.reshape(positions // 128, 128))
    return pl.pallas_call(
        write_out,
        out_shape=shapes,
        in_specs=[pl.BlockSpec(memory_space=pltpu.VMEM)] * 3,
        out_specs=[pl.BlockSpec(memory_space=pl.ANY)] * 3,
        scratch_shapes=[sem((3,))],
        name="write_out",
    )(*grads)


def solution(mesh):
    placed = P(("outer", "inner"), None)
    return jax.shard_map(
        local,
        mesh=mesh,
        in_specs=(placed, placed, placed, placed, P()),
        out_specs=(placed, placed, placed),
        check_vma=False,
    )
```

```python
import functools
import math

import jax
import jax.numpy as jnp
from jax import lax
from jax.experimental import pallas as pl
from jax.experimental.pallas import tpu as pltpu
from jax.sharding import PartitionSpec as P

MESH = pl.DeviceIdType.MESH
NEGATIVE = -1e30
TINY = 1e-30
HD = 128
HEADS = 3
SPAN = 64
CHUNK = 512
WINDOW = 5
QTILE = 256
QSTEPS = HEADS * (CHUNK // QTILE)
SCALE = HD**-0.5
KAPPA = SCALE * math.log2(math.e)
f32 = jnp.float32
bf16 = jnp.bfloat16


def dot(a, b, dims):
    return lax.dot_general(a, b, ((dims[0], dims[1]), ((), ())), preferred_element_type=f32)


def kernel(
    slabs_per_group,
    slabs,
    docs,
    q_hbm,
    k_hbm,
    v_hbm,
    g_hbm,
    seg_hbm,
    dq_out,
    dk_out,
    dv_out,
    qd,
    qd_other,
    kv,
    kv_other,
    seg,
    bias,
    half_stat,
    e_buf,
    dp_buf,
    ds_buf,
    stat,
    dq_part,
    dq_sib,
    dq_sum,
    dq_recv,
    dkv_own,
    dkv_send,
    dkv_recv,
    near_sem,
    far_sem,
    local_sem,
    seg_sem,
    qd_send_sem,
    qd_recv_sem,
    swap_send_sem,
    swap_recv_sem,
    kv_send_sem,
    kv_recv_sem,
    stat_send_sem,
    stat_recv_sem,
    dq_sib_send_sem,
    dq_sib_recv_sem,
    dq_send_sem,
    dq_recv_sem,
    dkv_send_sem,
    dkv_recv_sem,
):
    chunks = 2 * slabs
    sent = []
    group = lax.axis_index("outer")
    inner = lax.axis_index("inner")
    place = inner % 8
    base = inner - place
    slab = group * slabs_per_group + inner // 8
    x = place // 2
    core = place % 2
    is_back = x // 2
    unit = jnp.where(is_back == 1, 3 - x, x)
    chunk = jnp.where(is_back == 1, chunks - 1 - slab, slab)
    other_chunk = chunks - 1 - chunk

    def in_slab(place_to):
        return (group, base + place_to)

    def holder(chunk_to, half=0, core_to=core):
        back = chunk_to // slabs
        slab_to = jnp.where(back == 1, chunks - 1 - chunk_to, chunk_to)
        x_to = jnp.where((back + half) % 2 == 1, 3 - unit, unit)
        return (
            slab_to // slabs_per_group,
            (slab_to % slabs_per_group) * 8 + x_to * 2 + core_to,
        )

    def block_of(place_of, back):
        return jnp.where(back == 1, 7 - place_of, place_of)

    def rows_of(block):
        return pl.ds(pl.multiple_of(block * SPAN, SPAN), SPAN)

    sibling = place + 1 - 2 * core
    partner = (3 - x) * 2 + core
    mate = (x + 1 - 2 * (x % 2)) * 2 + core
    far = (3 - (x + 1 - 2 * (x % 2))) * 2 + core
    own_block = block_of(place, is_back)
    own_rows = pl.ds(pl.multiple_of(is_back * SPAN, SPAN), SPAN)
    other_rows = pl.ds(pl.multiple_of((1 - is_back) * SPAN, SPAN), SPAN)

    locals_ = [
        pltpu.make_async_copy(k_hbm.at[own_rows], kv.at[0, 0, 0], local_sem.at[0]),
        pltpu.make_async_copy(v_hbm.at[own_rows], kv.at[0, 0, 1], local_sem.at[1]),
        pltpu.make_async_copy(k_hbm.at[other_rows], kv_other.at[0], local_sem.at[2]),
        pltpu.make_async_copy(v_hbm.at[other_rows], kv_other.at[1], local_sem.at[3]),
        pltpu.make_async_copy(q_hbm.at[other_rows], qd_other.at[0], local_sem.at[4]),
        pltpu.make_async_copy(g_hbm.at[other_rows], qd_other.at[1], local_sem.at[5]),
        pltpu.make_async_copy(q_hbm.at[own_rows], qd.at[0, rows_of(own_block)], local_sem.at[6]),
        pltpu.make_async_copy(g_hbm.at[own_rows], qd.at[1, rows_of(own_block)], local_sem.at[7]),
    ]
    for copy in locals_:
        copy.start()
    seg_copy = pltpu.make_async_copy(seg_hbm, seg, seg_sem)
    seg_copy.start()

    barrier = pltpu.get_barrier_semaphore()
    for k in (2, 3, 1, 4):

        @pl.when(chunk - k >= 0)
        def _():
            pl.semaphore_signal(
                barrier, inc=1, device_id=holder(chunk - k, 0, 1), device_id_type=MESH
            )

    for step in range(4):
        to_x = (x + step) % 4

        @pl.when((step > 0) | (core == 1))
        def _():
            pl.semaphore_signal(barrier, inc=1, device_id=in_slab(2 * to_x), device_id_type=MESH)

    later = jnp.minimum(chunks - 1 - chunk, WINDOW - 1)
    apart = chunk - other_chunk

    @pl.when(core == 0)
    def _():
        pl.semaphore_wait(barrier, 7)
        pl.semaphore_signal(near_sem, inc=1, device_id=in_slab(sibling), device_id_type=MESH)

    @pl.when(core == 1)
    def _():
        pl.semaphore_wait(near_sem, 1)

    for copy in locals_:
        copy.wait()

    def send(src, dst, send_sem, recv_sem, to):
        copy = pltpu.make_async_remote_copy(
            src_ref=src,
            dst_ref=dst,
            send_sem=send_sem,
            recv_sem=recv_sem,
            device_id=to,
            device_id_type=MESH,
        )
        copy.start()
        return copy

    def arrived(dst, recv_sem):
        pltpu.make_async_copy(dst, dst, recv_sem).wait()

    def qd_block(block):
        return qd.at[:, rows_of(block)]

    def send_block(src, block, sem, to):
        return send(src, qd_block(block), qd_send_sem.at[sem], qd_recv_sem.at[block], in_slab(to))

    sent.append(send(kv_other, kv.at[1, 0], swap_send_sem, swap_recv_sem, in_slab(partner)))

    def kv_copy(k, half):
        return pltpu.make_async_remote_copy(
            src_ref=kv.at[half, 0],
            dst_ref=kv.at[half, k],
            send_sem=kv_send_sem.at[half, k],
            recv_sem=kv_recv_sem.at[half, k],
            device_id=holder(chunk + k),
            device_id_type=MESH,
        )

    def kv_start(half):
        for k in (2, 3, 1, 4):

            @pl.when(chunk + k < chunks)
            def _():
                kv_copy(k, half).start()

    other_block = block_of(place, 1 - is_back)
    sent.append(send_block(qd_other, other_block, 0, far))
    sent.append(send_block(qd_block(own_block), own_block, 1, mate))
    sent.append(send_block(qd_other, other_block, 2, partner))
    sent.append(send_block(qd_block(own_block), own_block, 3, sibling))

    @pl.when(core == 1)
    def _():
        @pl.when(later > 0)
        def _():
            pl.semaphore_wait(barrier, 2 * later)

        pl.semaphore_signal(far_sem, inc=1, device_id=in_slab(sibling), device_id_type=MESH)

    @pl.when(core == 0)
    def _():
        pl.semaphore_wait(far_sem, 1)

    kv_start(0)
    arrived(kv.at[1, 0], swap_recv_sem)
    kv_start(1)

    for k in range(1, WINDOW):

        @pl.when(chunk - k < 0)
        def _():
            kv[:, k] = jnp.zeros((2,) + kv.shape[2:], bf16)

    seg_copy.wait()
    doc_ids = lax.broadcasted_iota(jnp.int32, (docs, 128), 0)

    def count(i, acc):
        rows = seg[pl.ds(pl.multiple_of(i * 8, 8), 8), :]
        for r in range(8):
            acc = acc + jnp.where(rows[r : r + 1, :] < doc_ids, 1.0, 0.0)
        return acc

    tally = lax.fori_loop(0, seg.shape[0] // 8, count, jnp.zeros((docs, 128), f32))
    firsts = jnp.sum(tally, axis=1, keepdims=True)
    query_pos = (lax.broadcasted_iota(jnp.int32, (1, CHUNK), 1) + chunk * CHUNK).astype(f32)
    starts = jnp.max(jnp.where(firsts <= query_pos, firsts, 0.0), axis=0, keepdims=True)
    row_ids = lax.broadcasted_iota(jnp.int32, (SPAN, QTILE), 0)
    for k in range(WINDOW):
        key_chunk = chunk - k
        back = (key_chunk + slabs) // slabs - 1
        for half in range(2):
            front_place = jnp.where(half == 0, unit, 3 - unit) * 2 + core
            back_place = jnp.where(half == 0, 3 - unit, unit) * 2 + core
            block = jnp.where(back == 1, 7 - back_place, front_place)
            key_pos = (row_ids + (key_chunk * CHUNK + block * SPAN)).astype(f32)
            for part in range(CHUNK // QTILE):
                lanes = slice(part * QTILE, (part + 1) * QTILE)
                allowed = (key_pos >= starts[:, lanes]) & (key_pos <= query_pos[:, lanes])
                at = (WINDOW * half + k) * SPAN
                bias[part, at : at + SPAN, :] = jnp.where(allowed, 0.0, NEGATIVE)

    for sem, source in ((4, mate), (5, partner), (6, far)):
        block = block_of(source, is_back)
        arrived(qd_block(block), qd_recv_sem.at[block])
        sent.append(send_block(qd_block(block), block, sem, sibling))
    for step in range(4):
        block = block_of((sibling + 2 * step) % 8, is_back)
        arrived(qd_block(block), qd_recv_sem.at[block])
    shard = 2 * unit + core

    def forward(half):
        at = slice(WINDOW * SPAN * half, WINDOW * SPAN * (half + 1))
        keys = kv[half, :, 0].reshape(WINDOW * SPAN, HD)
        values = kv[half, :, 1].reshape(WINDOW * SPAN, HD)
        for n in range(QSTEPS):
            head, part = n // 2, n % 2
            rows = slice(part * QTILE, (part + 1) * QTILE)
            lanes = slice(head * HD, (head + 1) * HD)
            s = dot(keys, qd[0, rows, lanes], ((1,), (1,))) + bias[part, at, :]
            dp = dot(values, qd[1, rows, lanes], ((1,), (1,)))
            top = jnp.max(s, axis=0, keepdims=True)
            e = jnp.exp2((s - top) * KAPPA)
            e_buf[n, at, :] = e
            dp_buf[n, at, :] = dp
            half_stat[half, 0, n : n + 1, :] = top
            half_stat[half, 1, n : n + 1, :] = jnp.sum(e, axis=0, keepdims=True)
            half_stat[half, 2, n : n + 1, :] = jnp.sum(e * dp, axis=0, keepdims=True)

    half_stat[...] = jnp.zeros(half_stat.shape, f32)
    for half in range(2):
        for k in range(1, WINDOW):

            @pl.when(chunk - k >= 0)
            def _():
                arrived(kv.at[half, k], kv_recv_sem.at[half, k])
        forward(half)
    def combined(parts):
        top = jnp.max(parts[:, 0], axis=0)
        factors = jnp.exp2((parts[:, 0] - top[None]) * KAPPA)
        return (
            top,
            jnp.sum(parts[:, 1] * factors, axis=0),
            jnp.sum(parts[:, 2] * factors, axis=0),
        )

    for i, row in enumerate(combined(half_stat[...])):
        stat[shard, i] = row
    for sem, to in ((0, mate), (1, sibling), (2, mate + 1 - 2 * core)):
        sent.append(
            send(
                stat.at[shard],
                stat.at[shard],
                stat_send_sem.at[sem],
                stat_recv_sem.at[shard],
                in_slab(to),
            )
        )
    for step in range(1, 4):
        peer = (shard + step) % 4
        arrived(stat.at[peer], stat_recv_sem.at[peer])
    top, total, slope = combined(stat[...])
    inverse = 1.0 / jnp.maximum(total, TINY)
    delta = slope * inverse
    ratios = [jnp.exp2((half_stat[half, 0] - top) * KAPPA) * inverse for half in range(2)]

    def dkv_copy(k, half):
        return pltpu.make_async_remote_copy(
            src_ref=dkv_send.at[k, half],
            dst_ref=dkv_recv.at[half, k],
            send_sem=dkv_send_sem.at[half, k],
            recv_sem=dkv_recv_sem.at[half, k],
            device_id=holder(chunk - k, half),
            device_id_type=MESH,
        )
    for k in (2, 3, 1, 4, 0):
        dk = jnp.zeros((2 * SPAN, HD), f32)
        dv = jnp.zeros((2 * SPAN, HD), f32)
        for n in range(QSTEPS):
            head, part = n // 2, n % 2
            rows = slice(part * QTILE, (part + 1) * QTILE)
            lanes = slice(head * HD, (head + 1) * HD)
            p_halves, ds_halves = [], []
            for half in range(2):
                at = slice((WINDOW * half + k) * SPAN, (WINDOW * half + k + 1) * SPAN)
                p = e_buf[n, at, :] * ratios[half][n : n + 1]
                ds = (p * (dp_buf[n, at, :] - delta[n : n + 1])).astype(bf16)
                ds_buf[n, at, :] = ds
                p_halves.append(p.astype(bf16))
                ds_halves.append(ds)
            p = jnp.concatenate(p_halves, axis=0)
            ds = jnp.concatenate(ds_halves, axis=0)
            dv = dv + dot(p, qd[1, rows, lanes], ((1,), (0,)))
            dk = dk + dot(ds, qd[0, rows, lanes], ((1,), (0,)))
        dk = dk * SCALE
        if k == 0:
            dkv_own[0] = dk[:SPAN]
            dkv_own[1] = dv[:SPAN]
            dkv_send[0, 1, 0] = dk[SPAN:].astype(bf16)
            dkv_send[0, 1, 1] = dv[SPAN:].astype(bf16)
            sent.append(
                send(
                    dkv_send.at[0, 1],
                    dkv_recv.at[1, 0],
                    dkv_send_sem.at[1, 0],
                    dkv_recv_sem.at[1, 0],
                    in_slab(partner),
                )
            )
        else:
            dkv_send[k, :, 0] = dk.astype(bf16).reshape(2, SPAN, HD)
            dkv_send[k, :, 1] = dv.astype(bf16).reshape(2, SPAN, HD)

            @pl.when(chunk - k >= 0)
            def _():
                dkv_copy(k, 0).start()

            @pl.when((chunk - k >= 0) & (apart != k))
            def _():
                dkv_copy(k, 1).start()

            @pl.when(apart == k)
            def _():
                dkv_recv[1, k] = dkv_send[k, 1]
    keys = kv[:, :, 0].reshape(2 * SPAN * WINDOW, HD)
    for n in range(QSTEPS):
        head, part = n // 2, n % 2
        dqt = dot(keys, ds_buf[n], ((0,), (0,)))
        rows_dq = (dqt.T * SCALE).astype(bf16)
        for piece in range(QTILE // SPAN):
            owner = block_of(part * (QTILE // SPAN) + piece, is_back)
            dq_part[owner % 2, owner // 2, :, head * HD : (head + 1) * HD] = rows_dq[
                piece * SPAN : (piece + 1) * SPAN
            ]
    sent.append(send(dq_part.at[1 - core], dq_sib, dq_sib_send_sem, dq_sib_recv_sem, in_slab(sibling)))
    arrived(dq_sib, dq_sib_recv_sem)
    for step in (2, 1, 3, 0):
        to_x = (x + step) % 4
        dq_sum[step] = (dq_part[core, to_x].astype(f32) + dq_sib[to_x].astype(f32)).astype(bf16)
        if step > 0:
            sent.append(
                send(
                    dq_sum.at[step],
                    dq_recv.at[is_back, unit],
                    dq_send_sem.at[step],
                    dq_recv_sem.at[is_back, unit],
                    in_slab(2 * to_x + core),
                )
            )
    dq_recv[is_back, unit] = dq_sum[0]
    for step in range(1, 4):
        source_x = (x + step) % 4
        source_back = source_x // 2
        source_unit = jnp.where(source_back == 1, 3 - source_x, source_x)
        arrived(
            dq_recv.at[source_back, source_unit], dq_recv_sem.at[source_back, source_unit]
        )
    for back in range(2):
        total_dq = dq_recv[back, 0].astype(f32) + dq_recv[back, 1].astype(f32)
        dq_out[back * SPAN : (back + 1) * SPAN, :] = total_dq.astype(bf16)
    def add_arrived(half, there, k, total):
        @pl.when(there & (apart != k) if half == 1 else there)
        def _():
            arrived(dkv_recv.at[half, k], dkv_recv_sem.at[half, k])

        @pl.when(there)
        def _():
            total[...] = total[...] + dkv_recv[half, k].astype(f32)

    for k in range(4, 0, -1):
        add_arrived(0, chunk + k < chunks, k, dkv_own)
    dk_out[own_rows, :] = dkv_own[0].astype(bf16)
    dv_out[own_rows, :] = dkv_own[1].astype(bf16)
    arrived(dkv_recv.at[1, 0], dkv_recv_sem.at[1, 0])
    dkv_own[...] = dkv_recv[1, 0].astype(f32)
    for k in range(4, 0, -1):
        add_arrived(1, other_chunk + k < chunks, k, dkv_own)
    dk_out[other_rows, :] = dkv_own[0].astype(bf16)
    dv_out[other_rows, :] = dkv_own[1].astype(bf16)
    for copy in sent:
        copy.wait_send()
    for k in range(1, WINDOW):

        @pl.when(chunk + k < chunks)
        def _():
            for half in range(2):
                kv_copy(k, half).wait_send()
    for k in range(1, WINDOW):

        @pl.when(chunk - k >= 0)
        def _():
            dkv_copy(k, 0).wait_send()

        @pl.when((chunk - k >= 0) & (apart != k))
        def _():
            dkv_copy(k, 1).wait_send()


def write_out(dq, dk, dv, dq_out, dk_out, dv_out, sems):
    copies = [
        pltpu.make_async_copy(src, dst, sems.at[i])
        for i, (src, dst) in enumerate(((dq, dq_out), (dk, dk_out), (dv, dv_out)))
    ]
    for copy in copies:
        copy.start()
    for copy in copies:
        copy.wait()


def local(queries, key_rows, value_rows, grad_output, segments):
    groups = lax.axis_size("outer")
    slabs_per_group = lax.axis_size("inner") // 8
    slabs = groups * slabs_per_group
    rows = queries.shape[0]
    positions = segments.shape[0]
    vmem = pltpu.VMEM
    sem = pltpu.SemaphoreType.DMA
    keys = 2 * SPAN * WINDOW
    shapes = (
        jax.ShapeDtypeStruct((rows, HEADS * HD), bf16),
        jax.ShapeDtypeStruct((rows, HD), bf16),
        jax.ShapeDtypeStruct((rows, HD), bf16),
    )
    grads = pl.pallas_call(
        functools.partial(kernel, slabs_per_group, slabs, 32),
        out_shape=tuple(pltpu.VMEM(shape.shape, shape.dtype) for shape in shapes),
        in_specs=[pl.BlockSpec(memory_space=pl.ANY)] * 5,
        out_specs=[pl.BlockSpec(memory_space=pltpu.VMEM)] * 3,
        scratch_shapes=[
            vmem((2, CHUNK, HEADS * HD), bf16),
            vmem((2, SPAN, HEADS * HD), bf16),
            vmem((2, WINDOW, 2, SPAN, HD), bf16),
            vmem((2, SPAN, HD), bf16),
            vmem((positions // 128, 128), jnp.int32),
            vmem((CHUNK // QTILE, keys, QTILE), f32),
            vmem((2, 3, 8, QTILE), f32),
            vmem((QSTEPS, keys, QTILE), f32),
            vmem((QSTEPS, keys, QTILE), f32),
            vmem((QSTEPS, keys, QTILE), bf16),
            vmem((4, 3, 8, QTILE), f32),
            vmem((2, 4, SPAN, HEADS * HD), bf16),
            vmem((4, SPAN, HEADS * HD), bf16),
            vmem((4, SPAN, HEADS * HD), bf16),
            vmem((2, 2, SPAN, HEADS * HD), bf16),
            vmem((2, SPAN, HD), f32),
            vmem((WINDOW, 2, 2, SPAN, HD), bf16),
            vmem((2, WINDOW, 2, SPAN, HD), bf16),
            pltpu.SemaphoreType.REGULAR,
            pltpu.SemaphoreType.REGULAR,
            sem((8,)),
            sem,
            sem((7,)),
            sem((8,)),
            sem,
            sem,
            sem((2, WINDOW)),
            sem((2, WINDOW)),
            sem((3,)),
            sem((4,)),
            sem,
            sem,
            sem((4,)),
            sem((2, 2)),
            sem((2, WINDOW)),
            sem((2, WINDOW)),
        ],
        compiler_params=pltpu.CompilerParams(
            collective_id=0, has_side_effects=True, vmem_limit_bytes=60 * 1024 * 1024
        ),
        name="windowed_backward",
    )(queries, key_rows, value_rows, grad_output, segments.reshape(positions // 128, 128))
    return pl.pallas_call(
        write_out,
        out_shape=shapes,
        in_specs=[pl.BlockSpec(memory_space=pltpu.VMEM)] * 3,
        out_specs=[pl.BlockSpec(memory_space=pl.ANY)] * 3,
        scratch_shapes=[sem((3,))],
        name="write_out",
    )(*(pltpu.with_memory_space_constraint(grad, pltpu.VMEM) for grad in grads))


def solution(mesh):
    placed = P(("outer", "inner"), None)
    return jax.shard_map(
        local,
        mesh=mesh,
        in_specs=(placed, placed, placed, placed, P()),
        out_specs=(placed, placed, placed),
        check_vma=False,
    )
```

```python
import functools
import math

import jax
import jax.numpy as jnp
from jax import lax
from jax.experimental import pallas as pl
from jax.experimental.pallas import tpu as pltpu
from jax.sharding import PartitionSpec as P

MESH = pl.DeviceIdType.MESH
NEGATIVE = -1e30
TINY = 1e-30
HD = 128
HEADS = 3
SPAN = 64
CHUNK = 512
WINDOW = 5
QTILE = 256
QSTEPS = HEADS * (CHUNK // QTILE)
SCALE = HD**-0.5
KAPPA = SCALE * math.log2(math.e)
f32 = jnp.float32
bf16 = jnp.bfloat16


def dot(a, b, dims):
    return lax.dot_general(a, b, ((dims[0], dims[1]), ((), ())), preferred_element_type=f32)


def kernel(
    slabs_per_group,
    slabs,
    docs,
    q_hbm,
    k_hbm,
    v_hbm,
    g_hbm,
    seg_hbm,
    dq_out,
    dk_out,
    dv_out,
    qd,
    qd_other,
    kv,
    kv_other,
    seg,
    bias,
    half_stat,
    e_buf,
    dp_buf,
    ds_buf,
    stat,
    dq_part,
    dq_sib,
    dq_sum,
    dq_recv,
    dkv_own,
    dkv_send,
    dkv_recv,
    near_sem,
    far_sem,
    local_sem,
    seg_sem,
    qd_send_sem,
    qd_recv_sem,
    swap_send_sem,
    swap_recv_sem,
    kv_send_sem,
    kv_recv_sem,
    stat_send_sem,
    stat_recv_sem,
    dq_sib_send_sem,
    dq_sib_recv_sem,
    dq_send_sem,
    dq_recv_sem,
    dkv_send_sem,
    dkv_recv_sem,
):
    chunks = 2 * slabs
    sent = []
    group = lax.axis_index("outer")
    inner = lax.axis_index("inner")
    place = inner % 8
    base = inner - place
    slab = group * slabs_per_group + inner // 8
    x = place // 2
    core = place % 2
    is_back = x // 2
    unit = jnp.where(is_back == 1, 3 - x, x)
    chunk = jnp.where(is_back == 1, chunks - 1 - slab, slab)
    other_chunk = chunks - 1 - chunk

    def in_slab(place_to):
        return (group, base + place_to)

    def holder(chunk_to, half=0, core_to=core):
        back = chunk_to // slabs
        slab_to = jnp.where(back == 1, chunks - 1 - chunk_to, chunk_to)
        x_to = jnp.where((back + half) % 2 == 1, 3 - unit, unit)
        return (
            slab_to // slabs_per_group,
            (slab_to % slabs_per_group) * 8 + x_to * 2 + core_to,
        )

    def block_of(place_of, back):
        return jnp.where(back == 1, 7 - place_of, place_of)

    def rows_of(block):
        return pl.ds(pl.multiple_of(block * SPAN, SPAN), SPAN)

    sibling = place + 1 - 2 * core
    partner = (3 - x) * 2 + core
    mate = (x + 1 - 2 * (x % 2)) * 2 + core
    far = (3 - (x + 1 - 2 * (x % 2))) * 2 + core
    own_block = block_of(place, is_back)
    own_rows = pl.ds(pl.multiple_of(is_back * SPAN, SPAN), SPAN)
    other_rows = pl.ds(pl.multiple_of((1 - is_back) * SPAN, SPAN), SPAN)

    locals_ = [
        pltpu.make_async_copy(k_hbm.at[own_rows], kv.at[0, 0, 0], local_sem.at[0]),
        pltpu.make_async_copy(v_hbm.at[own_rows], kv.at[0, 0, 1], local_sem.at[1]),
        pltpu.make_async_copy(k_hbm.at[other_rows], kv_other.at[0], local_sem.at[2]),
        pltpu.make_async_copy(v_hbm.at[other_rows], kv_other.at[1], local_sem.at[3]),
        pltpu.make_async_copy(q_hbm.at[other_rows], qd_other.at[0], local_sem.at[4]),
        pltpu.make_async_copy(g_hbm.at[other_rows], qd_other.at[1], local_sem.at[5]),
        pltpu.make_async_copy(q_hbm.at[own_rows], qd.at[0, rows_of(own_block)], local_sem.at[6]),
        pltpu.make_async_copy(g_hbm.at[own_rows], qd.at[1, rows_of(own_block)], local_sem.at[7]),
    ]
    barrier = pltpu.get_barrier_semaphore()
    for k in (2, 3, 1, 4):

        @pl.when(chunk - k >= 0)
        def _():
            pl.semaphore_signal(
                barrier, inc=1, device_id=holder(chunk - k, 0, 1), device_id_type=MESH
            )

    for step in range(4):
        to_x = (x + step) % 4

        @pl.when((step > 0) | (core == 1))
        def _():
            pl.semaphore_signal(barrier, inc=1, device_id=in_slab(2 * to_x), device_id_type=MESH)

    for copy in locals_:
        copy.start()
    seg_copy = pltpu.make_async_copy(seg_hbm, seg, seg_sem)
    seg_copy.start()

    later = jnp.minimum(chunks - 1 - chunk, WINDOW - 1)
    apart = chunk - other_chunk

    @pl.when(core == 0)
    def _():
        pl.semaphore_wait(barrier, 7)
        pl.semaphore_signal(near_sem, inc=1, device_id=in_slab(sibling), device_id_type=MESH)

    @pl.when(core == 1)
    def _():
        pl.semaphore_wait(near_sem, 1)

    for copy in locals_:
        copy.wait()

    def send(src, dst, send_sem, recv_sem, to):
        copy = pltpu.make_async_remote_copy(
            src_ref=src,
            dst_ref=dst,
            send_sem=send_sem,
            recv_sem=recv_sem,
            device_id=to,
            device_id_type=MESH,
        )
        copy.start()
        return copy

    def arrived(dst, recv_sem):
        pltpu.make_async_copy(dst, dst, recv_sem).wait()

    def qd_block(block):
        return qd.at[:, rows_of(block)]

    def send_block(src, block, sem, to):
        return send(src, qd_block(block), qd_send_sem.at[sem], qd_recv_sem.at[block], in_slab(to))

    sent.append(send(kv_other, kv.at[1, 0], swap_send_sem, swap_recv_sem, in_slab(partner)))

    def kv_copy(k, half):
        return pltpu.make_async_remote_copy(
            src_ref=kv.at[half, 0],
            dst_ref=kv.at[half, k],
            send_sem=kv_send_sem.at[half, k],
            recv_sem=kv_recv_sem.at[half, k],
            device_id=holder(chunk + k),
            device_id_type=MESH,
        )

    def kv_start(half):
        for k in (2, 3, 1, 4):

            @pl.when(chunk + k < chunks)
            def _():
                kv_copy(k, half).start()

    other_block = block_of(place, 1 - is_back)
    sent.append(send_block(qd_other, other_block, 2, partner))
    sent.append(send_block(qd_block(own_block), own_block, 1, mate))
    sent.append(send_block(qd_other, other_block, 0, far))
    sent.append(send_block(qd_block(own_block), own_block, 3, sibling))

    @pl.when(core == 1)
    def _():
        @pl.when(later > 0)
        def _():
            pl.semaphore_wait(barrier, 2 * later)

        pl.semaphore_signal(far_sem, inc=1, device_id=in_slab(sibling), device_id_type=MESH)

    @pl.when(core == 0)
    def _():
        pl.semaphore_wait(far_sem, 1)

    kv_start(0)
    arrived(kv.at[1, 0], swap_recv_sem)
    kv_start(1)

    for k in range(1, WINDOW):

        @pl.when(chunk - k < 0)
        def _():
            kv[:, k] = jnp.zeros((2,) + kv.shape[2:], bf16)

    seg_copy.wait()
    doc_ids = lax.broadcasted_iota(jnp.int32, (docs, 128), 0)

    def count(i, acc):
        rows = seg[pl.ds(pl.multiple_of(i * 8, 8), 8), :]
        for r in range(8):
            acc = acc + jnp.where(rows[r : r + 1, :] < doc_ids, 1.0, 0.0)
        return acc

    tally = lax.fori_loop(0, seg.shape[0] // 8, count, jnp.zeros((docs, 128), f32))
    firsts = jnp.sum(tally, axis=1, keepdims=True)
    query_pos = (lax.broadcasted_iota(jnp.int32, (1, CHUNK), 1) + chunk * CHUNK).astype(f32)
    starts = jnp.max(jnp.where(firsts <= query_pos, firsts, 0.0), axis=0, keepdims=True)
    row_ids = lax.broadcasted_iota(jnp.int32, (SPAN, QTILE), 0)
    for k in range(WINDOW):
        key_chunk = chunk - k
        back = (key_chunk + slabs) // slabs - 1
        for half in range(2):
            front_place = jnp.where(half == 0, unit, 3 - unit) * 2 + core
            back_place = jnp.where(half == 0, 3 - unit, unit) * 2 + core
            block = jnp.where(back == 1, 7 - back_place, front_place)
            key_pos = (row_ids + (key_chunk * CHUNK + block * SPAN)).astype(f32)
            for part in range(CHUNK // QTILE):
                lanes = slice(part * QTILE, (part + 1) * QTILE)
                allowed = (key_pos >= starts[:, lanes]) & (key_pos <= query_pos[:, lanes])
                at = (WINDOW * half + k) * SPAN
                bias[part, at : at + SPAN, :] = jnp.where(allowed, 0.0, NEGATIVE)

    for sem, source in ((4, partner), (5, mate), (6, far)):
        block = block_of(source, is_back)
        arrived(qd_block(block), qd_recv_sem.at[block])
        sent.append(send_block(qd_block(block), block, sem, sibling))
    for step in range(4):
        block = block_of((sibling + 2 * step) % 8, is_back)
        arrived(qd_block(block), qd_recv_sem.at[block])
    shard = 2 * unit + core

    def forward(half):
        at = slice(WINDOW * SPAN * half, WINDOW * SPAN * (half + 1))
        keys = kv[half, :, 0].reshape(WINDOW * SPAN, HD)
        values = kv[half, :, 1].reshape(WINDOW * SPAN, HD)
        for n in range(QSTEPS):
            head, part = n // 2, n % 2
            rows = slice(part * QTILE, (part + 1) * QTILE)
            lanes = slice(head * HD, (head + 1) * HD)
            s = dot(keys, qd[0, rows, lanes], ((1,), (1,))) + bias[part, at, :]
            dp = dot(values, qd[1, rows, lanes], ((1,), (1,)))
            top = jnp.max(s, axis=0, keepdims=True)
            e = jnp.exp2((s - top) * KAPPA)
            e_buf[n, at, :] = e
            dp_buf[n, at, :] = dp
            half_stat[half, 0, n : n + 1, :] = top
            half_stat[half, 1, n : n + 1, :] = jnp.sum(e, axis=0, keepdims=True)
            half_stat[half, 2, n : n + 1, :] = jnp.sum(e * dp, axis=0, keepdims=True)

    half_stat[...] = jnp.zeros(half_stat.shape, f32)
    for half in range(2):
        for k in range(1, WINDOW):

            @pl.when(chunk - k >= 0)
            def _():
                arrived(kv.at[half, k], kv_recv_sem.at[half, k])
        forward(half)
    def combined(parts):
        top = jnp.max(parts[:, 0], axis=0)
        factors = jnp.exp2((parts[:, 0] - top[None]) * KAPPA)
        return (
            top,
            jnp.sum(parts[:, 1] * factors, axis=0),
            jnp.sum(parts[:, 2] * factors, axis=0),
        )

    for i, row in enumerate(combined(half_stat[...])):
        stat[shard, i] = row
    for sem, to in ((0, mate), (1, mate + 1 - 2 * core), (2, sibling)):
        sent.append(
            send(
                stat.at[shard],
                stat.at[shard],
                stat_send_sem.at[sem],
                stat_recv_sem.at[shard],
                in_slab(to),
            )
        )
    for step in range(1, 4):
        peer = (shard + step) % 4
        arrived(stat.at[peer], stat_recv_sem.at[peer])
    top, total, slope = combined(stat[...])
    inverse = 1.0 / jnp.maximum(total, TINY)
    delta = slope * inverse
    ratios = [jnp.exp2((half_stat[half, 0] - top) * KAPPA) * inverse for half in range(2)]

    def dkv_copy(k, half):
        return pltpu.make_async_remote_copy(
            src_ref=dkv_send.at[k, half],
            dst_ref=dkv_recv.at[half, k],
            send_sem=dkv_send_sem.at[half, k],
            recv_sem=dkv_recv_sem.at[half, k],
            device_id=holder(chunk - k, half),
            device_id_type=MESH,
        )
    for k in (3, 2, 1, 0, 4):
        dk = jnp.zeros((2 * SPAN, HD), f32)
        dv = jnp.zeros((2 * SPAN, HD), f32)
        for n in range(QSTEPS):
            head, part = n // 2, n % 2
            rows = slice(part * QTILE, (part + 1) * QTILE)
            lanes = slice(head * HD, (head + 1) * HD)
            p_halves, ds_halves = [], []
            for half in range(2):
                at = slice((WINDOW * half + k) * SPAN, (WINDOW * half + k + 1) * SPAN)
                p = e_buf[n, at, :] * ratios[half][n : n + 1]
                ds = (p * (dp_buf[n, at, :] - delta[n : n + 1])).astype(bf16)
                ds_buf[n, at, :] = ds
                p_halves.append(p.astype(bf16))
                ds_halves.append(ds)
            p = jnp.concatenate(p_halves, axis=0)
            ds = jnp.concatenate(ds_halves, axis=0)
            dv = dv + dot(p, qd[1, rows, lanes], ((1,), (0,)))
            dk = dk + dot(ds, qd[0, rows, lanes], ((1,), (0,)))
        dk = dk * SCALE
        if k == 0:
            dkv_own[0] = dk[:SPAN]
            dkv_own[1] = dv[:SPAN]
            dkv_send[0, 1, 0] = dk[SPAN:].astype(bf16)
            dkv_send[0, 1, 1] = dv[SPAN:].astype(bf16)
            sent.append(
                send(
                    dkv_send.at[0, 1],
                    dkv_recv.at[1, 0],
                    dkv_send_sem.at[1, 0],
                    dkv_recv_sem.at[1, 0],
                    in_slab(partner),
                )
            )
        else:
            dkv_send[k, :, 0] = dk.astype(bf16).reshape(2, SPAN, HD)
            dkv_send[k, :, 1] = dv.astype(bf16).reshape(2, SPAN, HD)

            @pl.when((chunk - k >= 0) & (apart != k))
            def _():
                dkv_copy(k, 1).start()

            @pl.when(chunk - k >= 0)
            def _():
                dkv_copy(k, 0).start()

            @pl.when(apart == k)
            def _():
                dkv_recv[1, k] = dkv_send[k, 1]
    keys = kv[:, :, 0].reshape(2 * SPAN * WINDOW, HD)
    for n in range(QSTEPS):
        head, part = n // 2, n % 2
        dqt = dot(keys, ds_buf[n], ((0,), (0,)))
        rows_dq = (dqt.T * SCALE).astype(bf16)
        for piece in range(QTILE // SPAN):
            owner = block_of(part * (QTILE // SPAN) + piece, is_back)
            dq_part[owner % 2, owner // 2, :, head * HD : (head + 1) * HD] = rows_dq[
                piece * SPAN : (piece + 1) * SPAN
            ]
    sent.append(send(dq_part.at[1 - core], dq_sib, dq_sib_send_sem, dq_sib_recv_sem, in_slab(sibling)))
    arrived(dq_sib, dq_sib_recv_sem)
    for step in (2, 1, 3, 0):
        to_x = (x + step) % 4
        dq_sum[step] = (dq_part[core, to_x].astype(f32) + dq_sib[to_x].astype(f32)).astype(bf16)
        if step > 0:
            sent.append(
                send(
                    dq_sum.at[step],
                    dq_recv.at[is_back, unit],
                    dq_send_sem.at[step],
                    dq_recv_sem.at[is_back, unit],
                    in_slab(2 * to_x + core),
                )
            )
    dq_recv[is_back, unit] = dq_sum[0]
    for step in range(1, 4):
        source_x = (x + step) % 4
        source_back = source_x // 2
        source_unit = jnp.where(source_back == 1, 3 - source_x, source_x)
        arrived(
            dq_recv.at[source_back, source_unit], dq_recv_sem.at[source_back, source_unit]
        )
    for back in range(2):
        total_dq = dq_recv[back, 0].astype(f32) + dq_recv[back, 1].astype(f32)
        dq_out[back * SPAN : (back + 1) * SPAN, :] = total_dq.astype(bf16)
    def add_arrived(half, there, k, total):
        @pl.when(there & (apart != k) if half == 1 else there)
        def _():
            arrived(dkv_recv.at[half, k], dkv_recv_sem.at[half, k])

        @pl.when(there)
        def _():
            total[...] = total[...] + dkv_recv[half, k].astype(f32)

    for k in range(4, 0, -1):
        add_arrived(0, chunk + k < chunks, k, dkv_own)
    dk_out[own_rows, :] = dkv_own[0].astype(bf16)
    dv_out[own_rows, :] = dkv_own[1].astype(bf16)
    arrived(dkv_recv.at[1, 0], dkv_recv_sem.at[1, 0])
    dkv_own[...] = dkv_recv[1, 0].astype(f32)
    for k in range(4, 0, -1):
        add_arrived(1, other_chunk + k < chunks, k, dkv_own)
    dk_out[other_rows, :] = dkv_own[0].astype(bf16)
    dv_out[other_rows, :] = dkv_own[1].astype(bf16)
    for copy in sent:
        copy.wait_send()
    for k in range(1, WINDOW):

        @pl.when(chunk + k < chunks)
        def _():
            for half in range(2):
                kv_copy(k, half).wait_send()
    for k in range(1, WINDOW):

        @pl.when(chunk - k >= 0)
        def _():
            dkv_copy(k, 0).wait_send()

        @pl.when((chunk - k >= 0) & (apart != k))
        def _():
            dkv_copy(k, 1).wait_send()


def write_out(dq, dk, dv, dq_out, dk_out, dv_out, sems):
    copies = [
        pltpu.make_async_copy(src, dst, sems.at[i])
        for i, (src, dst) in enumerate(((dq, dq_out), (dk, dk_out), (dv, dv_out)))
    ]
    for copy in copies:
        copy.start()
    for copy in copies:
        copy.wait()


def local(queries, key_rows, value_rows, grad_output, segments):
    groups = lax.axis_size("outer")
    slabs_per_group = lax.axis_size("inner") // 8
    slabs = groups * slabs_per_group
    rows = queries.shape[0]
    positions = segments.shape[0]
    vmem = pltpu.VMEM
    sem = pltpu.SemaphoreType.DMA
    keys = 2 * SPAN * WINDOW
    shapes = (
        jax.ShapeDtypeStruct((rows, HEADS * HD), bf16),
        jax.ShapeDtypeStruct((rows, HD), bf16),
        jax.ShapeDtypeStruct((rows, HD), bf16),
    )
    grads = pl.pallas_call(
        functools.partial(kernel, slabs_per_group, slabs, 32),
        out_shape=tuple(pltpu.VMEM(shape.shape, shape.dtype) for shape in shapes),
        in_specs=[pl.BlockSpec(memory_space=pl.ANY)] * 5,
        out_specs=[pl.BlockSpec(memory_space=pltpu.VMEM)] * 3,
        scratch_shapes=[
            vmem((2, CHUNK, HEADS * HD), bf16),
            vmem((2, SPAN, HEADS * HD), bf16),
            vmem((2, WINDOW, 2, SPAN, HD), bf16),
            vmem((2, SPAN, HD), bf16),
            vmem((positions // 128, 128), jnp.int32),
            vmem((CHUNK // QTILE, keys, QTILE), f32),
            vmem((2, 3, 8, QTILE), f32),
            vmem((QSTEPS, keys, QTILE), f32),
            vmem((QSTEPS, keys, QTILE), f32),
            vmem((QSTEPS, keys, QTILE), bf16),
            vmem((4, 3, 8, QTILE), f32),
            vmem((2, 4, SPAN, HEADS * HD), bf16),
            vmem((4, SPAN, HEADS * HD), bf16),
            vmem((4, SPAN, HEADS * HD), bf16),
            vmem((2, 2, SPAN, HEADS * HD), bf16),
            vmem((2, SPAN, HD), f32),
            vmem((WINDOW, 2, 2, SPAN, HD), bf16),
            vmem((2, WINDOW, 2, SPAN, HD), bf16),
            pltpu.SemaphoreType.REGULAR,
            pltpu.SemaphoreType.REGULAR,
            sem((8,)),
            sem,
            sem((7,)),
            sem((8,)),
            sem,
            sem,
            sem((2, WINDOW)),
            sem((2, WINDOW)),
            sem((3,)),
            sem((4,)),
            sem,
            sem,
            sem((4,)),
            sem((2, 2)),
            sem((2, WINDOW)),
            sem((2, WINDOW)),
        ],
        compiler_params=pltpu.CompilerParams(
            collective_id=0, has_side_effects=True, vmem_limit_bytes=60 * 1024 * 1024
        ),
        name="windowed_backward",
    )(queries, key_rows, value_rows, grad_output, segments.reshape(positions // 128, 128))
    return pl.pallas_call(
        write_out,
        out_shape=shapes,
        in_specs=[pl.BlockSpec(memory_space=pltpu.VMEM)] * 3,
        out_specs=[pl.BlockSpec(memory_space=pl.ANY)] * 3,
        scratch_shapes=[sem((3,))],
        name="write_out",
    )(*(pltpu.with_memory_space_constraint(grad, pltpu.VMEM) for grad in grads))


def solution(mesh):
    placed = P(("outer", "inner"), None)
    return jax.shard_map(
        local,
        mesh=mesh,
        in_specs=(placed, placed, placed, placed, P()),
        out_specs=(placed, placed, placed),
        check_vma=False,
    )
```

```python
import functools
import math

import jax
import jax.numpy as jnp
from jax import lax
from jax.experimental import pallas as pl
from jax.experimental.pallas import tpu as pltpu
from jax.sharding import PartitionSpec as P

MESH = pl.DeviceIdType.MESH
NEGATIVE = -1e30
TINY = 1e-30
HD = 128
HEADS = 3
SPAN = 64
CHUNK = 512
WINDOW = 5
QTILE = 256
QSTEPS = HEADS * (CHUNK // QTILE)
SCALE = HD**-0.5
KAPPA = SCALE * math.log2(math.e)
f32 = jnp.float32
bf16 = jnp.bfloat16


def dot(a, b, dims):
    return lax.dot_general(a, b, ((dims[0], dims[1]), ((), ())), preferred_element_type=f32)


def kernel(
    slabs_per_group,
    slabs,
    docs,
    q_hbm,
    k_hbm,
    v_hbm,
    g_hbm,
    seg_hbm,
    dq_out,
    dk_out,
    dv_out,
    qd,
    qd_other,
    kv,
    kv_other,
    seg,
    bias,
    half_stat,
    e_buf,
    dp_buf,
    ds_buf,
    stat,
    dq_part,
    dq_sib,
    dq_sum,
    dq_recv,
    dkv_own,
    dkv_send,
    dkv_recv,
    keys_t,
    near_sem,
    far_sem,
    local_sem,
    seg_sem,
    qd_send_sem,
    qd_recv_sem,
    swap_send_sem,
    swap_recv_sem,
    kv_send_sem,
    kv_recv_sem,
    stat_send_sem,
    stat_recv_sem,
    dq_sib_send_sem,
    dq_sib_recv_sem,
    dq_send_sem,
    dq_recv_sem,
    dkv_send_sem,
    dkv_recv_sem,
):
    chunks = 2 * slabs
    sent = []
    group = lax.axis_index("outer")
    inner = lax.axis_index("inner")
    place = inner % 8
    base = inner - place
    slab = group * slabs_per_group + inner // 8
    x = place // 2
    core = place % 2
    is_back = x // 2
    unit = jnp.where(is_back == 1, 3 - x, x)
    chunk = jnp.where(is_back == 1, chunks - 1 - slab, slab)
    other_chunk = chunks - 1 - chunk

    def in_slab(place_to):
        return (group, base + place_to)

    def holder(chunk_to, half=0, core_to=core):
        back = chunk_to // slabs
        slab_to = jnp.where(back == 1, chunks - 1 - chunk_to, chunk_to)
        x_to = jnp.where((back + half) % 2 == 1, 3 - unit, unit)
        return (
            slab_to // slabs_per_group,
            (slab_to % slabs_per_group) * 8 + x_to * 2 + core_to,
        )

    def block_of(place_of, back):
        return jnp.where(back == 1, 7 - place_of, place_of)

    def rows_of(block):
        return pl.ds(pl.multiple_of(block * SPAN, SPAN), SPAN)

    sibling = place + 1 - 2 * core
    partner = (3 - x) * 2 + core
    mate = (x + 1 - 2 * (x % 2)) * 2 + core
    far = (3 - (x + 1 - 2 * (x % 2))) * 2 + core
    own_block = block_of(place, is_back)
    own_rows = pl.ds(pl.multiple_of(is_back * SPAN, SPAN), SPAN)
    other_rows = pl.ds(pl.multiple_of((1 - is_back) * SPAN, SPAN), SPAN)

    locals_ = [
        pltpu.make_async_copy(k_hbm.at[own_rows], kv.at[0, 0, 0], local_sem.at[0]),
        pltpu.make_async_copy(v_hbm.at[own_rows], kv.at[0, 0, 1], local_sem.at[1]),
        pltpu.make_async_copy(k_hbm.at[other_rows], kv_other.at[0], local_sem.at[2]),
        pltpu.make_async_copy(v_hbm.at[other_rows], kv_other.at[1], local_sem.at[3]),
        pltpu.make_async_copy(q_hbm.at[other_rows], qd_other.at[0], local_sem.at[4]),
        pltpu.make_async_copy(g_hbm.at[other_rows], qd_other.at[1], local_sem.at[5]),
        pltpu.make_async_copy(q_hbm.at[own_rows], qd.at[0, rows_of(own_block)], local_sem.at[6]),
        pltpu.make_async_copy(g_hbm.at[own_rows], qd.at[1, rows_of(own_block)], local_sem.at[7]),
    ]
    barrier = pltpu.get_barrier_semaphore()
    for k in (2, 3, 1, 4):

        @pl.when(chunk - k >= 0)
        def _():
            pl.semaphore_signal(
                barrier, inc=1, device_id=holder(chunk - k, 0, 1), device_id_type=MESH
            )

    for step in range(4):
        to_x = (x + step) % 4

        @pl.when((step > 0) | (core == 1))
        def _():
            pl.semaphore_signal(barrier, inc=1, device_id=in_slab(2 * to_x), device_id_type=MESH)

    for copy in locals_[2:] + locals_[:2]:
        copy.start()
    seg_copy = pltpu.make_async_copy(seg_hbm, seg, seg_sem)
    seg_copy.start()

    later = jnp.minimum(chunks - 1 - chunk, WINDOW - 1)
    apart = chunk - other_chunk

    @pl.when(core == 0)
    def _():
        pl.semaphore_wait(barrier, 7)
        pl.semaphore_signal(near_sem, inc=1, device_id=in_slab(sibling), device_id_type=MESH)

    @pl.when(core == 1)
    def _():
        pl.semaphore_wait(near_sem, 1)


    def send(src, dst, send_sem, recv_sem, to):
        copy = pltpu.make_async_remote_copy(
            src_ref=src,
            dst_ref=dst,
            send_sem=send_sem,
            recv_sem=recv_sem,
            device_id=to,
            device_id_type=MESH,
        )
        copy.start()
        return copy

    def arrived(dst, recv_sem):
        pltpu.make_async_copy(dst, dst, recv_sem).wait()

    def qd_block(block):
        return qd.at[:, rows_of(block)]

    def send_block(src, block, sem, to):
        return send(src, qd_block(block), qd_send_sem.at[sem], qd_recv_sem.at[block], in_slab(to))

    for copy in locals_[2:4]:
        copy.wait()
    sent.append(send(kv_other, kv.at[1, 0], swap_send_sem, swap_recv_sem, in_slab(partner)))

    def kv_copy(k, half):
        return pltpu.make_async_remote_copy(
            src_ref=kv.at[half, 0],
            dst_ref=kv.at[half, k],
            send_sem=kv_send_sem.at[half, k],
            recv_sem=kv_recv_sem.at[half, k],
            device_id=holder(chunk + k),
            device_id_type=MESH,
        )

    def kv_start(half):
        for k in (2, 3, 1, 4):

            @pl.when(chunk + k < chunks)
            def _():
                kv_copy(k, half).start()

    other_block = block_of(place, 1 - is_back)
    for copy in locals_[:2] + locals_[4:]:
        copy.wait()
    sent.append(send_block(qd_other, other_block, 2, partner))
    sent.append(send_block(qd_block(own_block), own_block, 1, mate))
    sent.append(send_block(qd_other, other_block, 0, far))
    sent.append(send_block(qd_block(own_block), own_block, 3, sibling))

    @pl.when(core == 1)
    def _():
        @pl.when(later > 0)
        def _():
            pl.semaphore_wait(barrier, 2 * later)

        pl.semaphore_signal(far_sem, inc=1, device_id=in_slab(sibling), device_id_type=MESH)

    @pl.when(core == 0)
    def _():
        pl.semaphore_wait(far_sem, 1)

    kv_start(0)
    arrived(kv.at[1, 0], swap_recv_sem)
    kv_start(1)

    for k in range(1, WINDOW):

        @pl.when(chunk - k < 0)
        def _():
            kv[:, k] = jnp.zeros((2,) + kv.shape[2:], bf16)

    seg_copy.wait()
    doc_ids = lax.broadcasted_iota(jnp.int32, (docs, 128), 0)

    def count(i, acc):
        rows = seg[pl.ds(pl.multiple_of(i * 8, 8), 8), :]
        for r in range(8):
            acc = acc + jnp.where(rows[r : r + 1, :] < doc_ids, 1.0, 0.0)
        return acc

    tally = lax.fori_loop(0, seg.shape[0] // 8, count, jnp.zeros((docs, 128), f32))
    firsts = jnp.sum(tally, axis=1, keepdims=True)
    query_pos = (lax.broadcasted_iota(jnp.int32, (1, CHUNK), 1) + chunk * CHUNK).astype(f32)
    starts = jnp.max(jnp.where(firsts <= query_pos, firsts, 0.0), axis=0, keepdims=True)
    row_ids = lax.broadcasted_iota(jnp.int32, (SPAN, QTILE), 0)
    for k in range(WINDOW):
        key_chunk = chunk - k
        back = (key_chunk + slabs) // slabs - 1
        for half in range(2):
            front_place = jnp.where(half == 0, unit, 3 - unit) * 2 + core
            back_place = jnp.where(half == 0, 3 - unit, unit) * 2 + core
            block = jnp.where(back == 1, 7 - back_place, front_place)
            key_pos = (row_ids + (key_chunk * CHUNK + block * SPAN)).astype(f32)
            for part in range(CHUNK // QTILE):
                lanes = slice(part * QTILE, (part + 1) * QTILE)
                allowed = (key_pos >= starts[:, lanes]) & (key_pos <= query_pos[:, lanes])
                at = (WINDOW * half + k) * SPAN
                bias[part, at : at + SPAN, :] = jnp.where(allowed, 0.0, NEGATIVE)

    for sem, source in ((4, partner), (5, mate), (6, far)):
        block = block_of(source, is_back)
        arrived(qd_block(block), qd_recv_sem.at[block])
        sent.append(send_block(qd_block(block), block, sem, sibling))
    for step in range(4):
        block = block_of((sibling + 2 * step) % 8, is_back)
        arrived(qd_block(block), qd_recv_sem.at[block])
    shard = 2 * unit + core

    def forward(half):
        at = slice(WINDOW * SPAN * half, WINDOW * SPAN * (half + 1))
        keys = kv[half, :, 0].reshape(WINDOW * SPAN, HD)
        values = kv[half, :, 1].reshape(WINDOW * SPAN, HD)
        for n in range(QSTEPS):
            head, part = n // 2, n % 2
            rows = slice(part * QTILE, (part + 1) * QTILE)
            lanes = slice(head * HD, (head + 1) * HD)
            s = dot(keys, qd[0, rows, lanes], ((1,), (1,))) + bias[part, at, :]
            dp = dot(values, qd[1, rows, lanes], ((1,), (1,)))
            top = jnp.max(s, axis=0, keepdims=True)
            e = jnp.exp2((s - top) * KAPPA)
            e_buf[n, at, :] = e
            dp_buf[n, at, :] = dp
            half_stat[half, 0, n : n + 1, :] = top
            half_stat[half, 1, n : n + 1, :] = jnp.sum(e, axis=0, keepdims=True)
            half_stat[half, 2, n : n + 1, :] = jnp.sum(e * dp, axis=0, keepdims=True)

    half_stat[...] = jnp.zeros(half_stat.shape, f32)
    for half in range(2):
        for k in range(1, WINDOW):

            @pl.when(chunk - k >= 0)
            def _():
                arrived(kv.at[half, k], kv_recv_sem.at[half, k])
        forward(half)
    def combined(parts):
        top = jnp.max(parts[:, 0], axis=0)
        factors = jnp.exp2((parts[:, 0] - top[None]) * KAPPA)
        return (
            top,
            jnp.sum(parts[:, 1] * factors, axis=0),
            jnp.sum(parts[:, 2] * factors, axis=0),
        )

    for i, row in enumerate(combined(half_stat[...])):
        stat[shard, i] = row
    for sem, to in ((0, mate), (1, mate + 1 - 2 * core), (2, sibling)):
        sent.append(
            send(
                stat.at[shard],
                stat.at[shard],
                stat_send_sem.at[sem],
                stat_recv_sem.at[shard],
                in_slab(to),
            )
        )
    keys_t[...] = kv[:, :, 0].reshape(2 * SPAN * WINDOW, HD).T
    for step in range(1, 4):
        peer = (shard + step) % 4
        arrived(stat.at[peer], stat_recv_sem.at[peer])
    top, total, slope = combined(stat[...])
    inverse = 1.0 / jnp.maximum(total, TINY)
    delta = slope * inverse
    ratios = [jnp.exp2((half_stat[half, 0] - top) * KAPPA) * inverse for half in range(2)]

    def dkv_copy(k, half):
        return pltpu.make_async_remote_copy(
            src_ref=dkv_send.at[k, half],
            dst_ref=dkv_recv.at[half, k],
            send_sem=dkv_send_sem.at[half, k],
            recv_sem=dkv_recv_sem.at[half, k],
            device_id=holder(chunk - k, half),
            device_id_type=MESH,
        )
    for k in (3, 2, 1, 0, 4):
        dk = jnp.zeros((2 * SPAN, HD), f32)
        dv = jnp.zeros((2 * SPAN, HD), f32)
        for n in range(QSTEPS):
            head, part = n // 2, n % 2
            rows = slice(part * QTILE, (part + 1) * QTILE)
            lanes = slice(head * HD, (head + 1) * HD)
            p_halves, ds_halves = [], []
            for half in range(2):
                at = slice((WINDOW * half + k) * SPAN, (WINDOW * half + k + 1) * SPAN)
                p = e_buf[n, at, :] * ratios[half][n : n + 1]
                ds = (p * (dp_buf[n, at, :] - delta[n : n + 1])).astype(bf16)
                ds_buf[n, at, :] = ds
                p_halves.append(p.astype(bf16))
                ds_halves.append(ds)
            p = jnp.concatenate(p_halves, axis=0)
            ds = jnp.concatenate(ds_halves, axis=0)
            dv = dv + dot(p, qd[1, rows, lanes], ((1,), (0,)))
            dk = dk + dot(ds, qd[0, rows, lanes], ((1,), (0,)))
        dk = dk * SCALE
        if k == 0:
            dkv_own[0] = dk[:SPAN]
            dkv_own[1] = dv[:SPAN]
            dkv_send[0, 1, 0] = dk[SPAN:].astype(bf16)
            dkv_send[0, 1, 1] = dv[SPAN:].astype(bf16)
            sent.append(
                send(
                    dkv_send.at[0, 1],
                    dkv_recv.at[1, 0],
                    dkv_send_sem.at[1, 0],
                    dkv_recv_sem.at[1, 0],
                    in_slab(partner),
                )
            )
        else:
            dkv_send[k, :, 0] = dk.astype(bf16).reshape(2, SPAN, HD)
            dkv_send[k, :, 1] = dv.astype(bf16).reshape(2, SPAN, HD)

            @pl.when((chunk - k >= 0) & (apart != k))
            def _():
                dkv_copy(k, 1).start()

            @pl.when(chunk - k >= 0)
            def _():
                dkv_copy(k, 0).start()

            @pl.when(apart == k)
            def _():
                dkv_recv[1, k] = dkv_send[k, 1]
    for n in range(QSTEPS):
        head, part = n // 2, n % 2
        dqt = dot(keys_t[...], ds_buf[n], ((1,), (0,)))
        rows_dq = (dqt.T * SCALE).astype(bf16)
        for piece in range(QTILE // SPAN):
            owner = block_of(part * (QTILE // SPAN) + piece, is_back)
            dq_part[owner % 2, owner // 2, :, head * HD : (head + 1) * HD] = rows_dq[
                piece * SPAN : (piece + 1) * SPAN
            ]
    sent.append(send(dq_part.at[1 - core], dq_sib, dq_sib_send_sem, dq_sib_recv_sem, in_slab(sibling)))
    arrived(dq_sib, dq_sib_recv_sem)
    for step in (2, 1, 3, 0):
        to_x = (x + step) % 4
        dq_sum[step] = (dq_part[core, to_x].astype(f32) + dq_sib[to_x].astype(f32)).astype(bf16)
        if step > 0:
            sent.append(
                send(
                    dq_sum.at[step],
                    dq_recv.at[is_back, unit],
                    dq_send_sem.at[step],
                    dq_recv_sem.at[is_back, unit],
                    in_slab(2 * to_x + core),
                )
            )
    dq_recv[is_back, unit] = dq_sum[0]
    for step in range(1, 4):
        source_x = (x + step) % 4
        source_back = source_x // 2
        source_unit = jnp.where(source_back == 1, 3 - source_x, source_x)
        arrived(
            dq_recv.at[source_back, source_unit], dq_recv_sem.at[source_back, source_unit]
        )
    for back in range(2):
        total_dq = dq_recv[back, 0].astype(f32) + dq_recv[back, 1].astype(f32)
        dq_out[back * SPAN : (back + 1) * SPAN, :] = total_dq.astype(bf16)
    def add_arrived(half, there, k, total):
        @pl.when(there & (apart != k) if half == 1 else there)
        def _():
            arrived(dkv_recv.at[half, k], dkv_recv_sem.at[half, k])

        @pl.when(there)
        def _():
            total[...] = total[...] + dkv_recv[half, k].astype(f32)

    for k in range(4, 0, -1):
        add_arrived(0, chunk + k < chunks, k, dkv_own)
    dk_out[own_rows, :] = dkv_own[0].astype(bf16)
    dv_out[own_rows, :] = dkv_own[1].astype(bf16)
    arrived(dkv_recv.at[1, 0], dkv_recv_sem.at[1, 0])
    dkv_own[...] = dkv_recv[1, 0].astype(f32)
    for k in range(4, 0, -1):
        add_arrived(1, other_chunk + k < chunks, k, dkv_own)
    dk_out[other_rows, :] = dkv_own[0].astype(bf16)
    dv_out[other_rows, :] = dkv_own[1].astype(bf16)
    for copy in sent:
        copy.wait_send()
    for k in range(1, WINDOW):

        @pl.when(chunk + k < chunks)
        def _():
            for half in range(2):
                kv_copy(k, half).wait_send()
    for k in range(1, WINDOW):

        @pl.when(chunk - k >= 0)
        def _():
            dkv_copy(k, 0).wait_send()

        @pl.when((chunk - k >= 0) & (apart != k))
        def _():
            dkv_copy(k, 1).wait_send()


def write_out(dq, dk, dv, dq_out, dk_out, dv_out, sems):
    copies = [
        pltpu.make_async_copy(src, dst, sems.at[i])
        for i, (src, dst) in enumerate(((dq, dq_out), (dk, dk_out), (dv, dv_out)))
    ]
    for copy in copies:
        copy.start()
    for copy in copies:
        copy.wait()


def local(queries, key_rows, value_rows, grad_output, segments):
    groups = lax.axis_size("outer")
    slabs_per_group = lax.axis_size("inner") // 8
    slabs = groups * slabs_per_group
    rows = queries.shape[0]
    positions = segments.shape[0]
    vmem = pltpu.VMEM
    sem = pltpu.SemaphoreType.DMA
    keys = 2 * SPAN * WINDOW
    shapes = (
        jax.ShapeDtypeStruct((rows, HEADS * HD), bf16),
        jax.ShapeDtypeStruct((rows, HD), bf16),
        jax.ShapeDtypeStruct((rows, HD), bf16),
    )
    grads = pl.pallas_call(
        functools.partial(kernel, slabs_per_group, slabs, 32),
        out_shape=tuple(pltpu.VMEM(shape.shape, shape.dtype) for shape in shapes),
        in_specs=[pl.BlockSpec(memory_space=pl.ANY)] * 5,
        out_specs=[pl.BlockSpec(memory_space=pltpu.VMEM)] * 3,
        scratch_shapes=[
            vmem((2, CHUNK, HEADS * HD), bf16),
            vmem((2, SPAN, HEADS * HD), bf16),
            vmem((2, WINDOW, 2, SPAN, HD), bf16),
            vmem((2, SPAN, HD), bf16),
            vmem((positions // 128, 128), jnp.int32),
            vmem((CHUNK // QTILE, keys, QTILE), f32),
            vmem((2, 3, 8, QTILE), f32),
            vmem((QSTEPS, keys, QTILE), f32),
            vmem((QSTEPS, keys, QTILE), f32),
            vmem((QSTEPS, keys, QTILE), bf16),
            vmem((4, 3, 8, QTILE), f32),
            vmem((2, 4, SPAN, HEADS * HD), bf16),
            vmem((4, SPAN, HEADS * HD), bf16),
            vmem((4, SPAN, HEADS * HD), bf16),
            vmem((2, 2, SPAN, HEADS * HD), bf16),
            vmem((2, SPAN, HD), f32),
            vmem((WINDOW, 2, 2, SPAN, HD), bf16),
            vmem((2, WINDOW, 2, SPAN, HD), bf16),
            vmem((HD, keys), bf16),
            pltpu.SemaphoreType.REGULAR,
            pltpu.SemaphoreType.REGULAR,
            sem((8,)),
            sem,
            sem((7,)),
            sem((8,)),
            sem,
            sem,
            sem((2, WINDOW)),
            sem((2, WINDOW)),
            sem((3,)),
            sem((4,)),
            sem,
            sem,
            sem((4,)),
            sem((2, 2)),
            sem((2, WINDOW)),
            sem((2, WINDOW)),
        ],
        compiler_params=pltpu.CompilerParams(
            collective_id=0, has_side_effects=True, vmem_limit_bytes=60 * 1024 * 1024
        ),
        name="windowed_backward",
    )(queries, key_rows, value_rows, grad_output, segments.reshape(positions // 128, 128))
    return pl.pallas_call(
        write_out,
        out_shape=shapes,
        in_specs=[pl.BlockSpec(memory_space=pltpu.VMEM)] * 3,
        out_specs=[pl.BlockSpec(memory_space=pl.ANY)] * 3,
        scratch_shapes=[sem((3,))],
        name="write_out",
    )(*(pltpu.with_memory_space_constraint(grad, pltpu.VMEM) for grad in grads))


def solution(mesh):
    placed = P(("outer", "inner"), None)
    return jax.shard_map(
        local,
        mesh=mesh,
        in_specs=(placed, placed, placed, placed, P()),
        out_specs=(placed, placed, placed),
        check_vma=False,
    )
```
